768 devices in a mesh: depth: 12 (over z), row: 4 (over y_hi, core), col: 16 (over x, y_lo).
Axes of the slice: x: 4, y: 8 (y_hi: 2, y_lo: 4; y = y_hi * 4 + y_lo), z: 12, core: 2. Of those that a mesh axis runs over, the one named last changes fastest.
Arguments:
- phase: float32 [12, 256, 2048], P('depth', 'row', 'col'), may hold values from -1.8 to 1.8
- tilt: int32 [2, 2], replicated, may hold values from -6 to 6
- intensity: float32 [2, 256, 2048], P(None, 'row', 'col'), may hold values from 0.3 to 1.5
Outputs:
- grad_phase: float32 [12, 256, 2048], P('depth', 'row', 'col')
- exit_waves: float32 [2, 12, 2, 256, 2048], P(None, 'depth', None, 'row', 'col')
The draws below stay inside these ranges and needn't reach their ends.
Inputs may be any that keep to these rules, and one draw needn't show every extreme that they name: `tilt`: whole numbers of phase cycles across the field.
All inputs are finite; a program needn't handle non-finite values.
Results may differ from the reference program's by a relative error of at most 0.0003.
Values sent between devices are 32-bit elements; how exact they have to be, the bound alone decides.
A program may use at most 32 MiB of HBM per device.

```python
import math
import jax
import jax.numpy as jnp
from jax import lax

BATCH = 2
HALO = 32
FRESNEL = 64
NX = 256
NY = 2048
SLICES = 12


def place_ends(result, rng, least, high):
    shape = result.shape
    place = [jax.random.randint(jax.random.fold_in(rng, axis), (), 0, shape[axis]) for axis in range(len(shape))]
    result = result.at[tuple(place)].set(least)
    longest = shape.index(max(shape))
    place[longest] = (place[longest] + 1) % shape[longest]
    return result.at[tuple(place)].set(high)


def block_levels(own_key, shape, cuts, least, largest):
    loudness = 1.0
    for dim, blocks in cuts:
        steps = jax.random.uniform(jax.random.fold_in(jax.random.fold_in(own_key, 6), dim), (blocks,), jnp.float32, least / len(cuts), largest / len(cuts))
        loudness = loudness * jnp.repeat(jnp.exp(steps), shape[dim] // blocks).reshape((-1,) + (1,) * (len(shape) - 1 - dim))
    return loudness


def bell_draw(stream_key, shape, deviation, most, cuts=(), kind=jnp.bfloat16):
    gain = block_levels(stream_key, shape, cuts, -0.22, 0.18) if cuts else 1.0
    drawn = jax.random.normal(stream_key, shape, jnp.float32) * deviation * gain
    return jnp.minimum(jnp.maximum(drawn, -most), most).astype(kind)


def setup_inputs(seed: int = 0) -> dict:
    keys = jax.random.split(jax.random.key(seed), 4)
    return {
        "phase": bell_draw(keys[0], (SLICES, NX, NY), 0.3, 1.8, ((0, 12), (1, 4), (2, 16)), jnp.float32),
        "tilt": place_ends(jax.random.randint(keys[1], (BATCH, 2), -6, 7), jax.random.fold_in(keys[1], 1), -6, 6).astype(jnp.int32),
        "intensity": jnp.clip(0.3 + 1.2 * jax.random.uniform(keys[2], (BATCH, NX, NY), jnp.float32) ** block_levels(keys[2], (BATCH, NX, NY), ((1, 4), (2, 16)), -0.2, 0.2), 0.3, 1.5),
    }


def kernel_taps():
    offset = jnp.arange(-HALO, HALO + 1).astype(jnp.float32)
    taper_dist = jnp.maximum(jnp.abs(offset) - 0.5 * HALO, 0.0)
    profile = jnp.cos(jnp.pi * taper_dist / (HALO + 2.0))
    weight = profile * profile / math.sqrt(FRESNEL)
    phase_angle = jnp.pi * offset * offset / FRESNEL
    return lax.complex(jnp.cos(phase_angle) * weight, jnp.sin(phase_angle) * weight)

def convolve_axis(current, kernel, axis_num):
    extent = current.shape[axis_num]
    fft_size = extent + 2 * HALO
    kernel_hat = jnp.fft.fft(kernel, fft_size)
    shaped = [1, 1]
    shaped[axis_num] = fft_size
    field_hat = jnp.fft.fft(current, fft_size, axis=axis_num)
    full_conv = jnp.fft.ifft(field_hat * kernel_hat.reshape(shaped), axis=axis_num)
    return lax.slice_in_dim(full_conv, HALO, HALO + extent, axis=axis_num)

def forward(phase_field, tilt):
    kernel = kernel_taps()
    row_pos = jnp.arange(NX).astype(jnp.float32)[:, None]
    col_pos = jnp.arange(NY).astype(jnp.float32)[None, :]
    tilt_f = tilt.astype(jnp.float32)
    results = []
    for tilt_index in range(BATCH):
        phase_angle = 2.0 * jnp.pi * (tilt_f[tilt_index, 0] * row_pos / NX + tilt_f[tilt_index, 1] * col_pos / NY)
        current = lax.complex(jnp.cos(phase_angle), jnp.sin(phase_angle))
        leaving = []
        for slice_index in range(SLICES):
            screen = lax.complex(jnp.cos(phase_field[slice_index]), jnp.sin(phase_field[slice_index]))
            current = current * screen
            current = convolve_axis(convolve_axis(current, kernel, 0), kernel, 1)
            leaving.append(jnp.stack([jnp.real(current), jnp.imag(current)]))
        results.append(jnp.stack(leaving))
    return jnp.stack(results)

def reference(phase, tilt, intensity):

    def misfit_loss(phase_field):
        exit_fields = forward(phase_field, tilt)
        final_wave = exit_fields[:, SLICES - 1]
        misfit = final_wave[:, 0] * final_wave[:, 0] + final_wave[:, 1] * final_wave[:, 1] - intensity
        return (0.5 * jnp.sum(misfit * misfit), exit_fields)
    loss_value, pullback, exit_fields = jax.vjp(misfit_loss, phase, has_aux=True)
    gradient = pullback(jnp.ones_like(loss_value))[0]
    return (gradient, exit_fields)
```

```python
import functools
import math

import jax
import jax.numpy as jnp
import numpy as np
from jax import lax
from jax.experimental import pallas as pl
from jax.experimental.pallas import tpu as pltpu
from jax.sharding import PartitionSpec as P

HALO = 32
FRESNEL = 64
WIDTH = 32
MESH = pl.DeviceIdType.MESH
F32 = jnp.float32
BF16 = jnp.bfloat16


def taps(offset):
    offset = offset.astype(np.float64)
    dist = np.maximum(np.abs(offset) - 0.5 * HALO, 0.0)
    profile = np.cos(np.pi * dist / (HALO + 2.0))
    weight = profile * profile / math.sqrt(FRESNEL)
    angle = np.pi * offset * offset / FRESNEL
    inside = np.abs(offset) <= HALO
    re = np.where(inside, np.cos(angle) * weight, 0.0).astype(np.float32)
    im = np.where(inside, np.sin(angle) * weight, 0.0).astype(np.float32)
    return re, im


def halves(matrix):
    high = matrix.astype(BF16)
    low = (matrix - high.astype(np.float32)).astype(BF16)
    return high, low


def matrices(rows):
    i = np.arange(rows)
    re, im = taps(i[None, :] - i[:, None])
    row_high, row_low = halves(np.concatenate([re, im], axis=1))

    out = np.arange(WIDTH)
    blocks = []
    for shift in (-WIDTH, 0, WIDTH):
        re, im = taps(out[:, None] - (out[None, :] + shift))
        blocks.append(np.concatenate([np.concatenate([re, -im], 1), np.concatenate([im, re], 1)], 0))
    mid = np.concatenate(halves(blocks[1]), 0)
    rim = np.concatenate(halves(np.concatenate([blocks[0], blocks[2]], 1)), 0)
    return row_high, row_low, mid, rim


def split(value):
    high = value.astype(BF16)
    return high, (value - high.astype(F32)).astype(BF16)


def dot(a, b):
    return jnp.dot(a, b, preferred_element_type=F32)


def cmul(a, b):
    ar, ai, br, bi = a[:WIDTH], a[WIDTH:], b[:WIDTH], b[WIDTH:]
    return jnp.concatenate([ar * br - ai * bi, ar * bi + ai * br], axis=0)


def kernel(
    depth, cols, y_lo, slices,
    phase, tilt, intensity, row_high, row_low, mid_m, rim_m,
    grad, waves,
    tile_out, tile_in, level_out, level_in, strip_out, phase_w, screens, entering, leaving, moved, halo, grads,
    wave_in, grad_in, wave_out, wave_tiles, grad_out, grad_tiles,
    tile_s, tile_r, level_s, level_r, strip_s, strip_r, halo_s, halo_r, leave_s, leave_r, grads_s, grads_r,
    wave_s, wave_r, gout_s, gout_r,
):
    z, row, col = lax.axis_index("depth"), lax.axis_index("row"), lax.axis_index("col")
    ring = 2 * y_lo
    strips = 4 * cols
    rows = 256
    steps = 2 * slices
    worker = z < 2

    def place(x, turn, core):
        y = turn + (x % 2) * (ring - 1 - 2 * turn)
        return (y // y_lo) * 2 + core, x * y_lo + y % y_lo

    def strip_place(s):
        chip = s // 2
        return place(chip // ring, chip % ring, s % 2)

    x = col // y_lo
    y = (row // 2) * y_lo + col % y_lo
    turn = y + (x % 2) * (ring - 1 - 2 * y)
    strip = 2 * (x * ring + turn) + row % 2
    part = 2 * (turn % 2) + row % 2
    home_col = x * y_lo + turn // 2
    part_places = [place(x, 2 * (col % y_lo) + q // 2, q % 2) for q in range(4)]
    left = strip_place(jnp.maximum(strip - 1, 0))
    right = strip_place(jnp.minimum(strip + 1, strips - 1))
    has_left = worker & (strip > 0)
    has_right = worker & (strip < strips - 1)

    def same(device):
        return (device[0] == z) & (device[1] == row) & (device[2] == col)

    def remote(src, dst, send, recv, device):
        return pltpu.make_async_remote_copy(
            src_ref=src, dst_ref=dst, send_sem=send, recv_sem=recv, device_id=device, device_id_type=MESH
        )

    def push(src, dst, send, recv, device):
        me = same(device)

        @pl.when(jnp.logical_not(me))
        def _():
            remote(src, dst, send, recv, device).start()

        @pl.when(me)
        def _():
            pltpu.make_async_copy(src, dst, recv).start()

    def sent(src, dst, send, recv, device):
        @pl.when(jnp.logical_not(same(device)))
        def _():
            remote(src, dst, send, recv, device).wait_send()

    def arrived(buffer, recv):
        pltpu.make_async_copy(buffer, buffer, recv).wait()

    barrier = pltpu.get_barrier_semaphore()

    def greet(condition, device):
        @pl.when(condition)
        def _():
            pl.semaphore_signal(barrier, inc=1, device_id=device, device_id_type=MESH)

        return condition.astype(jnp.int32)

    expected = jnp.int32(0)
    for q in range(4):
        device = (z,) + part_places[q]
        expected += greet(jnp.logical_not(same(device)), device)
    for r in range(4):
        device = (z, jnp.int32(r), home_col)
        expected += greet(jnp.logical_not(same(device)), device)
    for plane in range(depth):
        wanted = z != plane
        if plane >= 2:
            wanted = wanted & worker
        expected += greet(wanted, (jnp.int32(plane), row, col))
    expected += greet(has_left, (z,) + left)
    expected += greet(has_right, (z,) + right)

    lane = lax.broadcasted_iota(jnp.int32, (16, 128), 1)
    first = lane < 64

    def pack_tile(tile, out):
        turned = jnp.concatenate([tile, tile], axis=0).T
        for q in range(4):
            out[q] = jnp.where(first, turned[32 * q : 32 * q + 16], turned[32 * q + 16 : 32 * q + 32])

    def strip_of(pieces):
        sides = []
        for h in range(2):
            a, b = pieces[2 * h], pieces[2 * h + 1]
            top = jnp.where(first, a, pltpu.roll(b, 64, 1))
            low = jnp.where(first, pltpu.roll(a, 64, 1), b)
            sides.append(jnp.concatenate([top, low], axis=0))
        return jnp.concatenate(sides, axis=1)

    def pack_strip(value, r):
        block = value[:, 128 * (r // 2) : 128 * (r // 2) + 128]
        a, b = block[:16], block[16:]
        if r % 2 == 0:
            return jnp.where(first, a, pltpu.roll(b, 64, 1))
        return jnp.where(first, pltpu.roll(a, 64, 1), b)

    def tile_of(pieces):
        parts = []
        for piece in pieces:
            parts += [piece, pltpu.roll(piece, 64, 1)]
        return jnp.concatenate(parts, axis=0).T[:64]

    pack_tile(phase[0], tile_out)

    @pl.when(worker)
    def _():
        pack_tile(intensity[jnp.minimum(z, 1)], level_out)

    pl.semaphore_wait(barrier, expected)

    for q in range(4):
        push(tile_out.at[q], tile_in.at[row], tile_s.at[q], tile_r, (z,) + part_places[q])

    @pl.when(worker)
    def _():
        for q in range(4):
            push(level_out.at[q], level_in.at[row], level_s.at[q], level_r, (z,) + part_places[q])

    arrived(tile_in, tile_r)
    strip_out[...] = strip_of([tile_in[r] for r in range(4)])
    for b in range(2):
        push(strip_out, phase_w.at[z], strip_s.at[b], strip_r.at[z], (jnp.int32(b), row, col))

    def row_step(value):
        high, low = split(value)
        both = dot(jnp.concatenate([high, low], axis=0), row_high[...])
        full = both[:64] + (both[64:] + dot(high, row_low[...]))
        re = full[:WIDTH, :rows] - full[WIDTH:, rows:]
        im = full[WIDTH:, :rows] + full[:WIDTH, rows:]
        return jnp.concatenate([re, im], axis=0)

    def col_part(matrix, value):
        high, low = split(value)
        both = dot(matrix[...], high)
        return both[:64] + (both[64:] + dot(matrix[:64], low))

    def halo_copies(k):
        return (
            remote(moved.at[k], halo.at[k, pl.ds(64, 64)], halo_s.at[0, k], halo_r.at[1, k], (z,) + left),
            remote(moved.at[k], halo.at[k, pl.ds(0, 64)], halo_s.at[1, k], halo_r.at[0, k], (z,) + right),
        )

    def halo_start(k):
        to_left, to_right = halo_copies(k)
        pl.when(has_left)(to_left.start)
        pl.when(has_right)(to_right.start)

    def halo_wait(k):
        to_left, to_right = halo_copies(k)
        pl.when(has_left)(to_right.wait_recv)
        pl.when(has_right)(to_left.wait_recv)

    def halo_sent(k):
        to_left, to_right = halo_copies(k)
        pl.when(has_left)(to_left.wait_send)
        pl.when(has_right)(to_right.wait_send)

    def make_screen(j):
        arrived(phase_w.at[j], strip_r.at[j])
        angle = phase_w[j]
        screens[j] = jnp.concatenate([jnp.cos(angle), jnp.sin(angle)], axis=0)

    def leave_args(j):
        b = jnp.minimum(z, 1)
        return leaving.at[j], wave_in.at[b], leave_s.at[j], leave_r.at[b], (j, row, col)

    def grads_args(j):
        b = jnp.minimum(z, 1)
        return grads.at[j], grad_in.at[b], grads_s.at[j], grads_r.at[b], (j, row, col)

    @pl.when(worker)
    def _():
        b = jnp.minimum(z, 1)

        @pl.when(strip == 0)
        def _():
            @pl.loop(0, steps)
            def _(k):
                halo[k, pl.ds(0, 64)] = jnp.zeros((64, rows), F32)

        @pl.when(strip == strips - 1)
        def _():
            @pl.loop(0, steps)
            def _(k):
                halo[k, pl.ds(64, 64)] = jnp.zeros((64, rows), F32)

        shape = (WIDTH, rows)
        row_pos = lax.broadcasted_iota(jnp.int32, shape, 1).astype(F32)
        col_pos = (strip * WIDTH + lax.broadcasted_iota(jnp.int32, shape, 0)).astype(F32)
        t0, t1 = tilt[b, 0].astype(F32), tilt[b, 1].astype(F32)
        angle = 2.0 * jnp.pi * (t0 * row_pos / float(rows) + t1 * col_pos / float(strips * WIDTH))
        incident = jnp.concatenate([jnp.cos(angle), jnp.sin(angle)], axis=0)
        make_screen(0)
        start = cmul(screens[0], incident)
        entering[0] = start
        moved[0] = row_step(start)

        def forward(j, carry):
            halo_start(j)
            local = col_part(mid_m, moved[j])

            @pl.when(j > 0)
            def _():
                push(*leave_args(j - 1))

            make_screen(j + 1)
            halo_wait(j)
            wave = local + col_part(rim_m, halo[j])
            leaving[j] = wave
            after = cmul(screens[j + 1], wave)
            entering[j + 1] = after
            moved[j + 1] = row_step(after)
            return carry

        lax.fori_loop(0, slices - 1, forward, 0)

        last = slices - 1
        halo_start(last)
        local = col_part(mid_m, moved[last])
        if last > 0:
            push(*leave_args(jnp.int32(last - 1)))
        arrived(level_in, level_r)
        level = strip_of([level_in[r] for r in range(4)])
        halo_wait(last)
        wave = local + col_part(rim_m, halo[last])
        leaving[last] = wave
        re, im = wave[:WIDTH], wave[WIDTH:]
        misfit = 2.0 * (re * re + im * im - level)
        moved[slices] = row_step(jnp.concatenate([misfit * re, -(misfit * im)], axis=0))
        halo_start(slices)
        push(*leave_args(jnp.int32(last)))

        def gradient(j, pulled):
            source = entering[j]
            grads[j] = -(pulled[:WIDTH] * source[WIDTH:] + pulled[WIDTH:] * source[:WIDTH])

        def backward(k, carry):
            j = steps - 1 - k
            local = col_part(mid_m, moved[k])
            halo_wait(k)
            pulled = local + col_part(rim_m, halo[k])
            moved[k + 1] = row_step(cmul(screens[j], pulled))
            halo_start(k + 1)
            gradient(j, pulled)
            push(*grads_args(j))
            return carry

        lax.fori_loop(slices, steps - 1, backward, 0)
        local = col_part(mid_m, moved[steps - 1])
        halo_wait(steps - 1)
        gradient(0, local + col_part(rim_m, halo[steps - 1]))
        push(*grads_args(jnp.int32(0)))

    for b in range(2):
        arrived(wave_in.at[b], leave_r.at[b])
        for r in range(4):
            for c in range(2):
                wave_out[b, r, c] = pack_strip(wave_in[b, pl.ds(32 * c, 32)], r)
            push(wave_out.at[b, r], wave_tiles.at[b, part], wave_s.at[b, r], wave_r.at[b], (z, jnp.int32(r), home_col))
    for b in range(2):
        arrived(wave_tiles.at[b], wave_r.at[b])
        for c in range(2):
            waves[b, 0, c] = tile_of([wave_tiles[b, q, c] for q in range(4)])
    for b in range(2):
        arrived(grad_in.at[b], grads_r.at[b])
    total = grad_in[0] + grad_in[1]
    for r in range(4):
        grad_out[r] = pack_strip(total, r)
        push(grad_out.at[r], grad_tiles.at[part], gout_s.at[r], gout_r, (z, jnp.int32(r), home_col))
    arrived(grad_tiles, gout_r)
    grad[0] = tile_of([grad_tiles[q] for q in range(4)])

    for q in range(4):
        sent(tile_out.at[q], tile_in.at[row], tile_s.at[q], tile_r, (z,) + part_places[q])
        sent(grad_out.at[q], grad_tiles.at[part], gout_s.at[q], gout_r, (z, jnp.int32(q), home_col))
        for b in range(2):
            sent(wave_out.at[b, q], wave_tiles.at[b, part], wave_s.at[b, q], wave_r.at[b], (z, jnp.int32(q), home_col))
    for b in range(2):
        sent(strip_out, phase_w.at[z], strip_s.at[b], strip_r.at[z], (jnp.int32(b), row, col))

    @pl.when(worker)
    def _():
        for q in range(4):
            sent(level_out.at[q], level_in.at[row], level_s.at[q], level_r, (z,) + part_places[q])

        @pl.loop(0, steps)
        def _(k):
            halo_sent(k)

        @pl.loop(0, slices)
        def _(j):
            sent(*leave_args(j))
            sent(*grads_args(j))


def solution(mesh):
    depth, cols = mesh.shape["depth"], mesh.shape["col"]
    y_lo = 4 if cols % 4 == 0 else 1
    slices = depth
    steps = 2 * slices
    rows = 256
    constants = [jnp.asarray(m) for m in matrices(rows)]

    def body(phase, tilt, intensity):
        vmem = pl.BlockSpec(memory_space=pltpu.VMEM)
        dma = pltpu.SemaphoreType.DMA
        wave = (64, rows)
        flops = 2 * steps * 64 * rows * (3 * 512 + 3 * 192)
        return pl.pallas_call(
            functools.partial(kernel, depth, cols, y_lo, slices),
            out_shape=(
                jax.ShapeDtypeStruct((1, 64, 128), F32),
                jax.ShapeDtypeStruct((2, 1, 2, 64, 128), F32),
            ),
            in_specs=[vmem, pl.BlockSpec(memory_space=pltpu.SMEM)] + [vmem] * 5,
            out_specs=(vmem, vmem),
            scratch_shapes=[
                pltpu.VMEM((4, 16, 128), F32),
                pltpu.VMEM((4, 16, 128), F32),
                pltpu.VMEM((4, 16, 128), F32),
                pltpu.VMEM((4, 16, 128), F32),
                pltpu.VMEM((WIDTH, rows), F32),
                pltpu.VMEM((slices, WIDTH, rows), F32),
                pltpu.VMEM((slices,) + wave, F32),
                pltpu.VMEM((slices,) + wave, F32),
                pltpu.VMEM((slices,) + wave, F32),
                pltpu.VMEM((steps,) + wave, F32),
                pltpu.VMEM((steps, 128, rows), F32),
                pltpu.VMEM((slices, WIDTH, rows), F32),
                pltpu.VMEM((2,) + wave, F32),
                pltpu.VMEM((2, WIDTH, rows), F32),
                pltpu.VMEM((2, 4, 2, 16, 128), F32),
                pltpu.VMEM((2, 4, 2, 16, 128), F32),
                pltpu.VMEM((4, 16, 128), F32),
                pltpu.VMEM((4, 16, 128), F32),
                dma((4,)),
                dma,
                dma((4,)),
                dma,
                dma((2,)),
                dma((slices,)),
                dma((2, steps)),
                dma((2, steps)),
                dma((slices,)),
                dma((2,)),
                dma((slices,)),
                dma((2,)),
                dma((2, 4)),
                dma((2,)),
                dma((4,)),
                dma,
            ],
            compiler_params=pltpu.CompilerParams(
                collective_id=0, has_side_effects=True, vmem_limit_bytes=48 * 2**20
            ),
            cost_estimate=pl.CostEstimate(flops=flops, bytes_accessed=2**21, transcendentals=2**18),
        )(phase, tilt, intensity, *constants)

    placed = (P("depth", "row", "col"), P(), P(None, "row", "col"))
    return jax.shard_map(
        body,
        mesh=mesh,
        in_specs=placed,
        out_specs=(P("depth", "row", "col"), P(None, "depth", None, "row", "col")),
        check_vma=False,
    )
```

```python
import functools
import math

import jax
import jax.numpy as jnp
import numpy as np
from jax import lax
from jax.experimental import pallas as pl
from jax.experimental.pallas import tpu as pltpu
from jax.sharding import PartitionSpec as P

HALO = 32
FRESNEL = 64
WIDTH = 32
OWN = 4
RUN = 4
ROWS = 256
MESH = pl.DeviceIdType.MESH
F32 = jnp.float32
BF16 = jnp.bfloat16


def taps(offset):
    offset = offset.astype(np.float64)
    dist = np.maximum(np.abs(offset) - 0.5 * HALO, 0.0)
    profile = np.cos(np.pi * dist / (HALO + 2.0))
    weight = profile * profile / math.sqrt(FRESNEL)
    angle = np.pi * offset * offset / FRESNEL
    inside = np.abs(offset) <= HALO
    re = np.where(inside, np.cos(angle) * weight, 0.0).astype(np.float32)
    im = np.where(inside, np.sin(angle) * weight, 0.0).astype(np.float32)
    return re, im


def halves(matrix):
    high = matrix.astype(BF16)
    low = (matrix - high.astype(np.float32)).astype(BF16)
    return high, low


def matrices():
    i = np.arange(ROWS)
    re, im = taps(i[None, :] - i[:, None])
    row_high, row_low = halves(np.concatenate([re, im], axis=1))

    lines = []
    for o in range(2):
        out = WIDTH * o + np.arange(WIDTH)
        top, low = [], []
        for i in range(4):
            re, im = taps(out[:, None] - (WIDTH * (i - 1) + np.arange(WIDTH))[None, :])
            top += [re, -im]
            low += [im, re]
        lines += [np.concatenate(top, 1), np.concatenate(low, 1)]
    pair = np.concatenate(halves(np.concatenate(lines, 0)), 0)
    return row_high, row_low, pair


def split(value):
    high = value.astype(BF16)
    return high, (value - high.astype(F32)).astype(BF16)


def dot(a, b):
    return jnp.dot(a, b, preferred_element_type=F32)


def blocks_of(value):
    for g in range(value.shape[0] // 64):
        yield value[64 * g : 64 * g + 32], value[64 * g + 32 : 64 * g + 64]


def cmul(a, b):
    out = []
    for (ar, ai), (br, bi) in zip(blocks_of(a), blocks_of(b)):
        out += [ar * br - ai * bi, ar * bi + ai * br]
    return jnp.concatenate(out, axis=0)


def cos_sin(x):
    y = x * x
    c = F32(-1.0 / math.factorial(14))
    s = F32(-1.0 / math.factorial(15))
    for n in range(6, -1, -1):
        sign = -1.0 if n % 2 else 1.0
        c = c * y + F32(sign / math.factorial(2 * n))
        s = s * y + F32(sign / math.factorial(2 * n + 1))
    return c, s * x


def kernel(
    depth, cols, y_lo, slices,
    phase_h, tilt_h, intensity_h, row_high_h, row_low_h, pair_h,
    grad, waves,
    phase, tilt, intensity, row_high, row_low, pair,
    tiles_in, levels_in, wide_out, phase_w, screens, entering, leaving, spread, work, grads,
    wave_in, grad_in, wave_out, grad_out, grad_tiles,
    load_s, tile_s, tile_r, level_s, level_r, wide_s, wide_r, halo_s, halo_r, leave_s, wave_r, grads_s, gin_r,
    wout_s, wout_r, gout_s, gout_r,
):
    z, row, col = lax.axis_index("depth"), lax.axis_index("row"), lax.axis_index("col")
    ring = 2 * y_lo
    half = cols // ring
    rounds = slices // RUN
    rim = RUN - 1
    own_rows = 64 * OWN
    side = 64 * RUN

    loads = [
        pltpu.make_async_copy(src, dst, load_s.at[i])
        for i, (src, dst) in enumerate(
            (
                (phase_h, phase), (intensity_h, intensity), (tilt_h, tilt),
                (row_high_h, row_high), (row_low_h, row_low), (pair_h, pair),
            )
        )
    ]
    for load in loads:
        load.start()

    x = col // y_lo
    y = (row // 2) * y_lo + col % y_lo
    b = x // half
    place_x = x % half
    strip = place_x * ring + y + (place_x % 2) * (ring - 1 - 2 * y)
    hub = row % 2 == 0
    worker = hub & (z == 0)
    wide = z % RUN != 0

    def hub_place(tilt_index, s):
        sx = s // ring
        turn = s % ring
        hy = turn + (sx % 2) * (ring - 1 - 2 * turn)
        return (hy // y_lo) * 2, (tilt_index * half + sx) * y_lo + hy % y_lo

    def clamp(s):
        return jnp.minimum(jnp.maximum(s, 0), cols - 1)

    left = (z,) + hub_place(b, clamp(strip - 1))
    right = (z,) + hub_place(b, clamp(strip + 1))
    has_left = worker & (strip > 0)
    has_right = worker & (strip < cols - 1)

    def same(device):
        return (device[0] == z) & (device[1] == row) & (device[2] == col)

    def remote(src, dst, send, recv, device):
        return pltpu.make_async_remote_copy(
            src_ref=src, dst_ref=dst, send_sem=send, recv_sem=recv, device_id=device, device_id_type=MESH
        )

    def push(src, dst, send, recv, device):
        me = same(device)

        @pl.when(jnp.logical_not(me))
        def _():
            remote(src, dst, send, recv, device).start()

        @pl.when(me)
        def _():
            pltpu.make_async_copy(src, dst, recv).start()

    def sent(src, dst, send, recv, device):
        @pl.when(jnp.logical_not(same(device)))
        def _():
            remote(src, dst, send, recv, device).wait_send()

    def arrived(buffer, recv):
        pltpu.make_async_copy(buffer, buffer, recv).wait()

    def tile_hubs():
        for t in range(2):
            for d in range(3):
                s = col + 1 - d
                wanted = (s >= 0) & (s < cols)
                if d != 1:
                    wanted = wanted & wide
                yield t, d, wanted, (z,) + hub_place(t, clamp(s))

    def hub_tiles():
        for d in range(3):
            c = strip + d - 1
            wanted = hub & (c >= 0) & (c < cols)
            if d != 1:
                wanted = wanted & wide
            for r in range(4):
                yield wanted, (z, jnp.int32(r), clamp(c))

    barrier = pltpu.get_barrier_semaphore()

    def greet(condition, device):
        @pl.when(condition)
        def _():
            pl.semaphore_signal(barrier, inc=1, device_id=device, device_id_type=MESH)

        return condition.astype(jnp.int32)

    expected = jnp.int32(0)
    for _, _, wanted, device in tile_hubs():
        expected += greet(wanted & jnp.logical_not(same(device)), device)
    for wanted, device in hub_tiles():
        expected += greet(wanted & jnp.logical_not(same(device)), device)
    for plane in range(1, depth):
        expected += greet(worker, (jnp.int32(plane), row, col))
    expected += greet(hub & (z != 0), (jnp.int32(0), row, col))
    expected += greet(has_left, left)
    expected += greet(has_right, right)

    loads[0].wait()
    loads[1].wait()
    pl.semaphore_wait(barrier, expected)

    for t, d, wanted, device in tile_hubs():
        pl.when(wanted)(
            functools.partial(push, phase.at[0], tiles_in.at[d, row], tile_s.at[t, d], tile_r.at[d], device)
        )

    def level_args(t):
        return intensity.at[t], levels_in.at[row], level_s.at[t], level_r, (z,) + hub_place(t, col)

    @pl.when(z == 0)
    def _():
        for t in range(2):
            push(*level_args(t))

    def turn_tiles(tiles, h):
        return jnp.concatenate([tiles[2 * h], tiles[2 * h + 1]], axis=0).T

    def wide_copy():
        return remote(wide_out, phase_w.at[z], wide_s, wide_r.at[z], (jnp.int32(0), row, col))

    def own_copy():
        span = pl.ds(32 * rim, 32 * OWN)
        return remote(wide_out.at[span], phase_w.at[z, span], wide_s, wide_r.at[z], (jnp.int32(0), row, col))

    @pl.when(hub)
    def _():
        arrived(tiles_in.at[1], tile_r.at[1])

        @pl.when(worker)
        def _():
            for h in range(2):
                phase_w[0, 32 * rim : 32 * (rim + OWN), 128 * h : 128 * h + 128] = turn_tiles(tiles_in[1], h)

        @pl.when(z != 0)
        def _():
            for h in range(2):
                wide_out[32 * rim : 32 * (rim + OWN), 128 * h : 128 * h + 128] = turn_tiles(tiles_in[1], h)

            @pl.when(wide)
            def _():
                @pl.when(strip > 0)
                def _():
                    arrived(tiles_in.at[0], tile_r.at[0])
                    for h in range(2):
                        turned = turn_tiles(tiles_in[0], h)
                        wide_out[: 32 * rim, 128 * h : 128 * h + 128] = turned[128 - 32 * rim :]

                @pl.when(strip == 0)
                def _():
                    wide_out[: 32 * rim] = jnp.zeros((32 * rim, ROWS), F32)

                @pl.when(strip < cols - 1)
                def _():
                    arrived(tiles_in.at[2], tile_r.at[2])
                    for h in range(2):
                        turned = turn_tiles(tiles_in[2], h)
                        wide_out[32 * (rim + OWN) :, 128 * h : 128 * h + 128] = turned[: 32 * rim]

                @pl.when(strip == cols - 1)
                def _():
                    wide_out[32 * (rim + OWN) :] = jnp.zeros((32 * rim, ROWS), F32)

                wide_copy().start()

            @pl.when(jnp.logical_not(wide))
            def _():
                own_copy().start()

    for load in loads[2:]:
        load.wait()

    def row_step(value):
        high, low = split(value)
        full = dot(high, row_high[...]) + (dot(low, row_high[...]) + dot(high, row_low[...]))
        out = []
        for a, c in blocks_of(full):
            out += [a[:, :ROWS] - c[:, ROWS:], c[:, :ROWS] + a[:, ROWS:]]
        return jnp.concatenate(out, axis=0)

    def col_step(value):
        high, low = split(value)
        out = []
        for p in range(value.shape[0] // 128 - 1):
            h, l = high[128 * p : 128 * p + 256], low[128 * p : 128 * p + 256]
            both = dot(pair[...], h)
            out.append(both[:128] + (both[128:] + dot(pair[:128], l)))
        return jnp.concatenate(out, axis=0)

    def halo_copies(k):
        return (
            remote(
                spread.at[k, pl.ds(side, side)], spread.at[k, pl.ds(side + own_rows, side)],
                halo_s.at[0, k], halo_r.at[1, k], left,
            ),
            remote(
                spread.at[k, pl.ds(own_rows, side)], spread.at[k, pl.ds(0, side)],
                halo_s.at[1, k], halo_r.at[0, k], right,
            ),
        )

    def halo_start(k):
        to_left, to_right = halo_copies(k)
        pl.when(has_left)(to_left.start)
        pl.when(has_right)(to_right.start)

    def halo_wait(k):
        to_left, to_right = halo_copies(k)
        pl.when(has_left)(to_right.wait_recv)
        pl.when(has_right)(to_left.wait_recv)

    def halo_sent(k):
        to_left, to_right = halo_copies(k)
        pl.when(has_left)(to_left.wait_send)
        pl.when(has_right)(to_right.wait_send)

    def make_screen(j, with_rim):
        for g in range(0 if with_rim else rim, OWN + (2 * rim if with_rim else rim)):
            c, s = cos_sin(phase_w[j, 32 * g : 32 * g + 32])
            if g < rim:
                c, s = jnp.where(strip > 0, c, 0.0), jnp.where(strip > 0, s, 0.0)
            if g >= rim + OWN:
                c, s = jnp.where(strip < cols - 1, c, 0.0), jnp.where(strip < cols - 1, s, 0.0)
            screens[j, 64 * g : 64 * g + 32] = c
            screens[j, 64 * g + 32 : 64 * g + 64] = s

    def get_screen(j, with_rim):
        if with_rim:
            arrived(phase_w.at[j], wide_r.at[j])
        else:
            span = pl.ds(32 * rim, 32 * OWN)
            arrived(phase_w.at[j, span], wide_r.at[j])
        make_screen(j, with_rim)

    def screen_on(j, out):
        return screens[j, pl.ds(64 * (rim - out), 64 * (OWN + 2 * out))]

    def leave_args(j):
        return leaving.at[j], wave_in, leave_s.at[j], wave_r, (j, row, col)

    def grads_args(j):
        return grads.at[j], grad_in, grads_s.at[j], gin_r, (j, row, col)

    def leave_start(j):
        pl.when(j > 0)(remote(*leave_args(j)).start)

    def grads_start(j):
        pl.when(j > 0)(remote(*grads_args(j)).start)

    def wave_turn(src):
        for c in range(2):
            value = jnp.concatenate([src[64 * g + 32 * c : 64 * g + 32 * c + 32] for g in range(OWN)], axis=0)
            for h in range(2):
                turned = value[:, 128 * h : 128 * h + 128].T
                wave_out[2 * h, c] = turned[:64]
                wave_out[2 * h + 1, c] = turned[64:]
        for r in range(4):
            push(*wave_args(r))

    def wave_args(r):
        return wave_out.at[r], waves.at[b, 0], wout_s.at[r], wout_r.at[b], (z, jnp.int32(r), strip)

    def grad_turn(src):
        for h in range(2):
            turned = src[:, 128 * h : 128 * h + 128].T
            grad_out[2 * h] = turned[:64]
            grad_out[2 * h + 1] = turned[64:]
        for r in range(4):
            push(*grad_args(r))

    def grad_args(r):
        return grad_out.at[r], grad_tiles.at[b], gout_s.at[r], gout_r.at[b], (z, jnp.int32(r), strip)

    def next_input(i, k):
        return spread[k] if i == 1 else work[pl.ds(0, 64 * (OWN + 2 * (RUN - i + 1)))]

    def own_part(value, out):
        return value[64 * out : 64 * out + own_rows]

    def forward(k, last):
        first_slice = k * RUN
        halo_start(k)
        for i in range(1, RUN + (0 if last else 1)):
            get_screen(first_slice + i, i < RUN)
        halo_wait(k)
        for i in range(1, RUN + 1):
            out = RUN - i
            j = first_slice + i - 1
            wave = col_step(next_input(i, k))
            leaving[j] = own_part(wave, out)
            leave_start(j)
            if i < RUN:
                after = cmul(screen_on(j + 1, out), wave)
                entering[j + 1] = own_part(after, out)
                work[pl.ds(0, 64 * (OWN + 2 * out))] = row_step(after)
            elif not last:
                after = cmul(screen_on(j + 1, 0), wave)
                entering[j + 1] = after
                spread[k + 1, pl.ds(side, own_rows)] = row_step(after)
            else:
                arrived(levels_in, level_r)
                level = jnp.concatenate([turn_tiles(levels_in, h) for h in range(2)], axis=1)
                seed = []
                for g, (re, im) in enumerate(blocks_of(wave)):
                    misfit = 2.0 * (re * re + im * im - level[32 * g : 32 * g + 32])
                    seed += [misfit * re, -(misfit * im)]
                spread[k + 1, pl.ds(side, own_rows)] = row_step(jnp.concatenate(seed, axis=0))

    def backward(k, last):
        first_slice = (2 * rounds - k) * RUN - 1
        halo_wait(k)
        for i in range(1, RUN + 1):
            out = RUN - i
            j = first_slice - (i - 1)
            pulled = col_step(next_input(i, k))
            if i < RUN:
                work[pl.ds(0, 64 * (OWN + 2 * out))] = row_step(cmul(screen_on(j, out), pulled))
            elif not last:
                spread[k + 1, pl.ds(side, own_rows)] = row_step(cmul(screen_on(j, 0), pulled))
                halo_start(k + 1)
            parts = []
            for (pr, pi), (er, ei) in zip(blocks_of(own_part(pulled, out)), blocks_of(entering[j])):
                parts.append(-(pr * ei + pi * er))
            grads[j] = jnp.concatenate(parts, axis=0)
            grads_start(j)

    @pl.when(worker)
    def _():
        @pl.when(strip == 0)
        def _():
            @pl.loop(0, 2 * rounds)
            def _(k):
                spread[k, pl.ds(0, side)] = jnp.zeros((side, ROWS), F32)

        @pl.when(strip == cols - 1)
        def _():
            @pl.loop(0, 2 * rounds)
            def _(k):
                spread[k, pl.ds(side + own_rows, side)] = jnp.zeros((side, ROWS), F32)

        row_pos = lax.broadcasted_iota(jnp.int32, (32 * OWN, ROWS), 1).astype(F32)
        col_pos = (strip * (32 * OWN) + lax.broadcasted_iota(jnp.int32, (32 * OWN, ROWS), 0)).astype(F32)
        t0, t1 = tilt[b, 0].astype(F32), tilt[b, 1].astype(F32)
        angle = 2.0 * jnp.pi * (t0 * row_pos / float(ROWS) + t1 * col_pos / float(cols * 32 * OWN))
        cos, sin = jnp.cos(angle), jnp.sin(angle)
        incident = []
        for g in range(OWN):
            incident += [cos[32 * g : 32 * g + 32], sin[32 * g : 32 * g + 32]]
        make_screen(0, False)
        start = cmul(screen_on(0, 0), jnp.concatenate(incident, axis=0))
        entering[0] = start
        spread[0, pl.ds(side, own_rows)] = row_step(start)

        def forward_round(k, carry):
            forward(k, False)
            return carry

        def backward_round(k, carry):
            backward(k, False)
            return carry

        if rounds > 1:
            lax.fori_loop(0, rounds - 1, forward_round, 0)
        forward(jnp.int32(rounds - 1), True)
        halo_start(rounds)
        wave_turn(leaving.at[0])
        if rounds > 1:
            lax.fori_loop(rounds, 2 * rounds - 1, backward_round, 0)
        backward(jnp.int32(2 * rounds - 1), True)
        grad_turn(grads.at[0])

    @pl.when(hub & (z != 0))
    def _():
        arrived(wave_in, wave_r)
        wave_turn(wave_in)
        arrived(grad_in, gin_r)
        grad_turn(grad_in)

    for t in range(2):
        arrived(waves.at[t, 0], wout_r.at[t])
    for t in range(2):
        arrived(grad_tiles.at[t], gout_r.at[t])
    grad[0] = grad_tiles[0] + grad_tiles[1]

    for t, d, wanted, device in tile_hubs():
        pl.when(wanted)(
            functools.partial(sent, phase.at[0], tiles_in.at[d, row], tile_s.at[t, d], tile_r.at[d], device)
        )

    @pl.when(z == 0)
    def _():
        for t in range(2):
            sent(*level_args(t))

    @pl.when(hub)
    def _():
        for r in range(4):
            sent(*wave_args(r))
            sent(*grad_args(r))
        pl.when((z != 0) & wide)(wide_copy().wait_send)
        pl.when((z != 0) & jnp.logical_not(wide))(own_copy().wait_send)

    @pl.when(worker)
    def _():
        @pl.loop(0, 2 * rounds)
        def _(k):
            halo_sent(k)

        @pl.loop(1, slices)
        def _(j):
            remote(*leave_args(j)).wait_send()
            remote(*grads_args(j)).wait_send()


def solution(mesh):
    depth, cols = mesh.shape["depth"], mesh.shape["col"]
    y_lo = 4 if cols % 8 == 0 else 1
    slices = depth
    rounds = 2 * slices // RUN
    reach = OWN + 2 * (RUN - 1)
    constants = [jnp.asarray(m) for m in matrices()]

    def body(phase, tilt, intensity):
        hbm = pl.BlockSpec(memory_space=pltpu.HBM)
        vmem = pl.BlockSpec(memory_space=pltpu.VMEM)
        dma = pltpu.SemaphoreType.DMA
        strip = (64 * OWN, ROWS)
        flops = 2 * 2 * slices * 64 * 7 * ROWS * (3 * 512 + 3 * 256)
        return pl.pallas_call(
            functools.partial(kernel, depth, cols, y_lo, slices),
            out_shape=(
                jax.ShapeDtypeStruct((1, 64, 128), F32),
                jax.ShapeDtypeStruct((2, 1, 2, 64, 128), F32),
            ),
            in_specs=[hbm] * 6,
            out_specs=(vmem, vmem),
            scratch_shapes=[
                pltpu.VMEM((1, 64, 128), F32),
                pltpu.SMEM((2, 2), jnp.int32),
                pltpu.VMEM((2, 64, 128), F32),
                pltpu.VMEM((ROWS, 2 * ROWS), BF16),
                pltpu.VMEM((ROWS, 2 * ROWS), BF16),
                pltpu.VMEM((256, 256), BF16),
                pltpu.VMEM((3, 4, 64, 128), F32),
                pltpu.VMEM((4, 64, 128), F32),
                pltpu.VMEM((32 * reach, ROWS), F32),
                pltpu.VMEM((slices, 32 * reach, ROWS), F32),
                pltpu.VMEM((slices, 64 * reach, ROWS), F32),
                pltpu.VMEM((slices,) + strip, F32),
                pltpu.VMEM((slices,) + strip, F32),
                pltpu.VMEM((rounds, 64 * (OWN + 2 * RUN), ROWS), F32),
                pltpu.VMEM((64 * reach, ROWS), F32),
                pltpu.VMEM((slices, 32 * OWN, ROWS), F32),
                pltpu.VMEM(strip, F32),
                pltpu.VMEM((32 * OWN, ROWS), F32),
                pltpu.VMEM((4, 2, 64, 128), F32),
                pltpu.VMEM((4, 64, 128), F32),
                pltpu.VMEM((2, 64, 128), F32),
                dma((6,)),
                dma((2, 3)),
                dma((3,)),
                dma((2,)),
                dma,
                dma,
                dma((slices,)),
                dma((2, rounds)),
                dma((2, rounds)),
                dma((slices,)),
                dma,
                dma((slices,)),
                dma,
                dma((4,)),
                dma((2,)),
                dma((4,)),
                dma((2,)),
            ],
            compiler_params=pltpu.CompilerParams(
                collective_id=0, has_side_effects=True, vmem_limit_bytes=56 * 2**20
            ),
            cost_estimate=pl.CostEstimate(flops=flops, bytes_accessed=2**21, transcendentals=2**18),
        )(phase, tilt, intensity, *constants)

    placed = (P("depth", "row", "col"), P(), P(None, "row", "col"))
    return jax.shard_map(
        body,
        mesh=mesh,
        in_specs=placed,
        out_specs=(P("depth", "row", "col"), P(None, "depth", None, "row", "col")),
        check_vma=False,
    )
```

```python
import functools
import math

import jax
import jax.numpy as jnp
import numpy as np
from jax import lax
from jax.experimental import pallas as pl
from jax.experimental.pallas import tpu as pltpu
from jax.sharding import PartitionSpec as P

HALO = 32
FRESNEL = 64
WIDTH = 32
OWN = 4
RUN = 4
ROWS = 256
HOME = 2
MESH = pl.DeviceIdType.MESH
F32 = jnp.float32
BF16 = jnp.bfloat16


def taps(offset):
    offset = offset.astype(np.float64)
    dist = np.maximum(np.abs(offset) - 0.5 * HALO, 0.0)
    profile = np.cos(np.pi * dist / (HALO + 2.0))
    weight = profile * profile / math.sqrt(FRESNEL)
    angle = np.pi * offset * offset / FRESNEL
    inside = np.abs(offset) <= HALO
    re = np.where(inside, np.cos(angle) * weight, 0.0).astype(np.float32)
    im = np.where(inside, np.sin(angle) * weight, 0.0).astype(np.float32)
    return re, im


def halves(matrix):
    high = matrix.astype(BF16)
    low = (matrix - high.astype(np.float32)).astype(BF16)
    return high, low


def matrices():
    i = np.arange(ROWS)
    re, im = taps(i[None, :] - i[:, None])
    row_high, row_low = halves(np.concatenate([re, im], axis=1))

    lines = []
    for o in range(2):
        out = WIDTH * o + np.arange(WIDTH)
        top, low = [], []
        for i in range(4):
            re, im = taps(out[:, None] - (WIDTH * (i - 1) + np.arange(WIDTH))[None, :])
            top += [re, -im]
            low += [im, re]
        lines += [np.concatenate(top, 1), np.concatenate(low, 1)]
    pair = np.concatenate(halves(np.concatenate(lines, 0)), 0)
    return row_high, row_low, pair


def split(value):
    high = value.astype(BF16)
    return high, (value - high.astype(F32)).astype(BF16)


def dot(a, b):
    return jnp.dot(a, b, preferred_element_type=F32)


def blocks_of(value):
    for g in range(value.shape[0] // 64):
        yield value[64 * g : 64 * g + 32], value[64 * g + 32 : 64 * g + 64]


def cmul(a, b):
    out = []
    for (ar, ai), (br, bi) in zip(blocks_of(a), blocks_of(b)):
        out += [ar * br - ai * bi, ar * bi + ai * br]
    return jnp.concatenate(out, axis=0)


def cos_sin(x):
    y = x * x
    c = F32(-1.0 / math.factorial(14))
    s = F32(-1.0 / math.factorial(15))
    for n in range(6, -1, -1):
        sign = -1.0 if n % 2 else 1.0
        c = c * y + F32(sign / math.factorial(2 * n))
        s = s * y + F32(sign / math.factorial(2 * n + 1))
    return c, s * x


def kernel(
    depth, cols, y_lo, slices,
    phase_h, tilt_h, intensity_h, row_high_h, row_low_h, pair_h,
    grad, waves,
    phase, tilt, intensity, row_high, row_low, pair,
    tiles_in, levels_in, wide_out, phase_w, screens, entering, leaving, spread, work, grads,
    wave_in, grad_in, wave_out, grad_out, grad_tiles,
    load_s, tile_s, tile_r, level_s, level_r, wide_s, wide_r, halo_s, halo_r, leave_s, leave_r, wave_r,
    grads_s, grads_r, gin_r, wout_s, wout_r, gout_s, gout_r,
):
    z, row, col = lax.axis_index("depth"), lax.axis_index("row"), lax.axis_index("col")
    ring = 2 * y_lo
    half = cols // ring
    rounds = slices // RUN
    rim = RUN - 1
    own_rows = 64 * OWN
    side = 64 * RUN

    loads = [
        pltpu.make_async_copy(src, dst, load_s.at[i])
        for i, (src, dst) in enumerate(
            (
                (phase_h, phase), (intensity_h, intensity), (tilt_h, tilt),
                (row_high_h, row_high), (row_low_h, row_low), (pair_h, pair),
            )
        )
    ]
    for load in loads:
        load.start()

    x = col // y_lo
    y = (row // 2) * y_lo + col % y_lo
    b = x // half
    place_x = x % half
    strip = place_x * ring + y + (place_x % 2) * (ring - 1 - 2 * y)
    hub = row % 2 == 0
    home = min(HOME, depth - 1)
    worker = hub & (z == home)
    porter = jnp.logical_not(hub) & (z == home)
    base_row = row - row % 2
    wide = z % RUN != 0

    def hub_place(tilt_index, s):
        sx = s // ring
        turn = s % ring
        hy = turn + (sx % 2) * (ring - 1 - 2 * turn)
        return (hy // y_lo) * 2, (tilt_index * half + sx) * y_lo + hy % y_lo

    def clamp(s):
        return jnp.minimum(jnp.maximum(s, 0), cols - 1)

    left = (z,) + hub_place(b, clamp(strip - 1))
    right = (z,) + hub_place(b, clamp(strip + 1))
    has_left = worker & (strip > 0)
    has_right = worker & (strip < cols - 1)

    def same(device):
        return (device[0] == z) & (device[1] == row) & (device[2] == col)

    def remote(src, dst, send, recv, device):
        return pltpu.make_async_remote_copy(
            src_ref=src, dst_ref=dst, send_sem=send, recv_sem=recv, device_id=device, device_id_type=MESH
        )

    def push(src, dst, send, recv, device):
        me = same(device)

        @pl.when(jnp.logical_not(me))
        def _():
            remote(src, dst, send, recv, device).start()

        @pl.when(me)
        def _():
            pltpu.make_async_copy(src, dst, recv).start()

    def sent(src, dst, send, recv, device):
        @pl.when(jnp.logical_not(same(device)))
        def _():
            remote(src, dst, send, recv, device).wait_send()

    def arrived(buffer, recv):
        pltpu.make_async_copy(buffer, buffer, recv).wait()

    def tile_hubs():
        for t in range(2):
            for d in range(3):
                s = col + 1 - d
                wanted = (s >= 0) & (s < cols)
                if d != 1:
                    wanted = wanted & wide
                yield t, d, wanted, (z,) + hub_place(t, clamp(s))

    def hub_tiles():
        for d in range(3):
            c = strip + d - 1
            wanted = hub & (c >= 0) & (c < cols)
            if d != 1:
                wanted = wanted & wide
            for r in range(4):
                yield wanted, (z, jnp.int32(r), clamp(c))

    barrier = pltpu.get_barrier_semaphore()

    def greet(condition, device):
        @pl.when(condition)
        def _():
            pl.semaphore_signal(barrier, inc=1, device_id=device, device_id_type=MESH)

        return condition.astype(jnp.int32)

    expected = jnp.int32(0)
    for _, _, wanted, device in tile_hubs():
        expected += greet(wanted & jnp.logical_not(same(device)), device)
    for wanted, device in hub_tiles():
        expected += greet(wanted & jnp.logical_not(same(device)), device)
    for plane in range(depth):
        if plane != home:
            greet(worker, (jnp.int32(plane), row, col))
    away = hub & (z != home)
    greet(away, (jnp.int32(home), row + 1, col))
    greet(porter, (z, base_row, col))
    expected += (away | worker).astype(jnp.int32) + porter.astype(jnp.int32) * (depth - 1)
    expected += greet(has_left, left)
    expected += greet(has_right, right)

    loads[0].wait()
    loads[1].wait()
    pl.semaphore_wait(barrier, expected)

    for t, d, wanted, device in tile_hubs():
        pl.when(wanted)(
            functools.partial(push, phase.at[0], tiles_in.at[d, row], tile_s.at[t, d], tile_r.at[d], device)
        )

    def level_args(t):
        return intensity.at[t], levels_in.at[row], level_s.at[t], level_r, (z,) + hub_place(t, col)

    @pl.when(z == home)
    def _():
        for t in range(2):
            push(*level_args(t))

    def turn_tiles(tiles, h):
        return jnp.concatenate([tiles[2 * h], tiles[2 * h + 1]], axis=0).T

    def wide_args():
        return wide_out, phase_w.at[z], wide_s, wide_r.at[z], (jnp.int32(home), row, col)

    def own_args():
        span = pl.ds(32 * rim, 32 * OWN)
        return wide_out.at[span], phase_w.at[z, span], wide_s, wide_r.at[z], (jnp.int32(home), row, col)

    @pl.when(hub)
    def _():
        arrived(tiles_in.at[1], tile_r.at[1])
        for h in range(2):
            wide_out[32 * rim : 32 * (rim + OWN), 128 * h : 128 * h + 128] = turn_tiles(tiles_in[1], h)

        @pl.when(wide)
        def _():
            @pl.when(strip > 0)
            def _():
                arrived(tiles_in.at[0], tile_r.at[0])
                for h in range(2):
                    turned = turn_tiles(tiles_in[0], h)
                    wide_out[: 32 * rim, 128 * h : 128 * h + 128] = turned[128 - 32 * rim :]

            @pl.when(strip == 0)
            def _():
                wide_out[: 32 * rim] = jnp.zeros((32 * rim, ROWS), F32)

            @pl.when(strip < cols - 1)
            def _():
                arrived(tiles_in.at[2], tile_r.at[2])
                for h in range(2):
                    turned = turn_tiles(tiles_in[2], h)
                    wide_out[32 * (rim + OWN) :, 128 * h : 128 * h + 128] = turned[: 32 * rim]

            @pl.when(strip == cols - 1)
            def _():
                wide_out[32 * (rim + OWN) :] = jnp.zeros((32 * rim, ROWS), F32)

            push(*wide_args())

        @pl.when(jnp.logical_not(wide))
        def _():
            push(*own_args())

    for load in loads[2:]:
        load.wait()

    def row_step(value):
        high, low = split(value)
        full = dot(high, row_high[...]) + (dot(low, row_high[...]) + dot(high, row_low[...]))
        out = []
        for a, c in blocks_of(full):
            out += [a[:, :ROWS] - c[:, ROWS:], c[:, :ROWS] + a[:, ROWS:]]
        return jnp.concatenate(out, axis=0)

    def col_step(value):
        high, low = split(value)
        out = []
        for p in range(value.shape[0] // 128 - 1):
            h, l = high[128 * p : 128 * p + 256], low[128 * p : 128 * p + 256]
            both = dot(pair[...], h)
            out.append(both[:128] + (both[128:] + dot(pair[:128], l)))
        return jnp.concatenate(out, axis=0)

    def halo_copies(k):
        return (
            remote(
                spread.at[k, pl.ds(side, side)], spread.at[k, pl.ds(side + own_rows, side)],
                halo_s.at[0, k], halo_r.at[1, k], left,
            ),
            remote(
                spread.at[k, pl.ds(own_rows, side)], spread.at[k, pl.ds(0, side)],
                halo_s.at[1, k], halo_r.at[0, k], right,
            ),
        )

    def halo_start(k):
        to_left, to_right = halo_copies(k)
        pl.when(has_left)(to_left.start)
        pl.when(has_right)(to_right.start)

    def halo_wait(k):
        to_left, to_right = halo_copies(k)
        pl.when(has_left)(to_right.wait_recv)
        pl.when(has_right)(to_left.wait_recv)

    def halo_sent(k):
        to_left, to_right = halo_copies(k)
        pl.when(has_left)(to_left.wait_send)
        pl.when(has_right)(to_right.wait_send)

    def make_screen(j, with_rim):
        for g in range(0 if with_rim else rim, OWN + (2 * rim if with_rim else rim)):
            c, s = cos_sin(phase_w[j, 32 * g : 32 * g + 32])
            if g < rim:
                c, s = jnp.where(strip > 0, c, 0.0), jnp.where(strip > 0, s, 0.0)
            if g >= rim + OWN:
                c, s = jnp.where(strip < cols - 1, c, 0.0), jnp.where(strip < cols - 1, s, 0.0)
            screens[j, 64 * g : 64 * g + 32] = c
            screens[j, 64 * g + 32 : 64 * g + 64] = s

    def get_screen(j, with_rim):
        if with_rim:
            arrived(phase_w.at[j], wide_r.at[j])
        else:
            span = pl.ds(32 * rim, 32 * OWN)
            arrived(phase_w.at[j, span], wide_r.at[j])
        make_screen(j, with_rim)

    def screen_on(j, out):
        return screens[j, pl.ds(64 * (rim - out), 64 * (OWN + 2 * out))]

    def leave_copy(j):
        return remote(leaving.at[j], leaving.at[j], leave_s.at[j], leave_r.at[j], (z, base_row + 1, col))

    def grads_copy(j):
        return remote(grads.at[j], grads.at[j], grads_s.at[j], grads_r.at[j], (z, base_row + 1, col))

    def leave_carry(j):
        return remote(leaving.at[j], wave_in, leave_s.at[j], wave_r, (j, base_row, col))

    def grads_carry(j):
        return remote(grads.at[j], grad_in, grads_s.at[j], gin_r, (j, base_row, col))

    def leave_start(j):
        pl.when(j != home)(leave_copy(j).start)

    def grads_start(j):
        pl.when(j != home)(grads_copy(j).start)

    def wave_turn(src):
        for c in range(2):
            value = jnp.concatenate([src[64 * g + 32 * c : 64 * g + 32 * c + 32] for g in range(OWN)], axis=0)
            for h in range(2):
                turned = value[:, 128 * h : 128 * h + 128].T
                wave_out[2 * h, c] = turned[:64]
                wave_out[2 * h + 1, c] = turned[64:]
        for r in range(4):
            push(*wave_args(r))

    def wave_args(r):
        return wave_out.at[r], waves.at[b, 0], wout_s.at[r], wout_r.at[b], (z, jnp.int32(r), strip)

    def grad_turn(src):
        for h in range(2):
            turned = src[:, 128 * h : 128 * h + 128].T
            grad_out[2 * h] = turned[:64]
            grad_out[2 * h + 1] = turned[64:]
        for r in range(4):
            push(*grad_args(r))

    def grad_args(r):
        return grad_out.at[r], grad_tiles.at[b], gout_s.at[r], gout_r.at[b], (z, jnp.int32(r), strip)

    def next_input(i, k):
        return spread[k] if i == 1 else work[pl.ds(0, 64 * (OWN + 2 * (RUN - i + 1)))]

    def own_part(value, out):
        return value[64 * out : 64 * out + own_rows]

    def forward(k, last):
        first_slice = k * RUN
        halo_start(k)
        pl.when(k > 0)(lambda: leave_start(first_slice - 1))
        for i in range(1, RUN + (0 if last else 1)):
            get_screen(first_slice + i, i < RUN)
        halo_wait(k)
        for i in range(1, RUN + 1):
            out = RUN - i
            j = first_slice + i - 1
            wave = col_step(next_input(i, k))
            leaving[j] = own_part(wave, out)
            if i < RUN:
                leave_start(j)
                after = cmul(screen_on(j + 1, out), wave)
                entering[j + 1] = own_part(after, out)
                work[pl.ds(0, 64 * (OWN + 2 * out))] = row_step(after)
            elif not last:
                after = cmul(screen_on(j + 1, 0), wave)
                entering[j + 1] = after
                spread[k + 1, pl.ds(side, own_rows)] = row_step(after)
            else:
                arrived(levels_in, level_r)
                level = jnp.concatenate([turn_tiles(levels_in, h) for h in range(2)], axis=1)
                seed = []
                for g, (re, im) in enumerate(blocks_of(wave)):
                    misfit = 2.0 * (re * re + im * im - level[32 * g : 32 * g + 32])
                    seed += [misfit * re, -(misfit * im)]
                spread[k + 1, pl.ds(side, own_rows)] = row_step(jnp.concatenate(seed, axis=0))

    def backward(k, last):
        first_slice = (2 * rounds - k) * RUN - 1
        halo_wait(k)
        for i in range(1, RUN + 1):
            out = RUN - i
            j = first_slice - (i - 1)
            pulled = col_step(next_input(i, k))
            if i < RUN:
                work[pl.ds(0, 64 * (OWN + 2 * out))] = row_step(cmul(screen_on(j, out), pulled))
            elif not last:
                spread[k + 1, pl.ds(side, own_rows)] = row_step(cmul(screen_on(j, 0), pulled))
                halo_start(k + 1)
            parts = []
            for (pr, pi), (er, ei) in zip(blocks_of(own_part(pulled, out)), blocks_of(entering[j])):
                parts.append(-(pr * ei + pi * er))
            grads[j] = jnp.concatenate(parts, axis=0)
            grads_start(j)

    @pl.when(worker)
    def _():
        @pl.when(strip == 0)
        def _():
            @pl.loop(0, 2 * rounds)
            def _(k):
                spread[k, pl.ds(0, side)] = jnp.zeros((side, ROWS), F32)

        @pl.when(strip == cols - 1)
        def _():
            @pl.loop(0, 2 * rounds)
            def _(k):
                spread[k, pl.ds(side + own_rows, side)] = jnp.zeros((side, ROWS), F32)

        row_pos = lax.broadcasted_iota(jnp.int32, (32 * OWN, ROWS), 1).astype(F32)
        col_pos = (strip * (32 * OWN) + lax.broadcasted_iota(jnp.int32, (32 * OWN, ROWS), 0)).astype(F32)
        t0, t1 = tilt[b, 0].astype(F32), tilt[b, 1].astype(F32)
        angle = 2.0 * jnp.pi * (t0 * row_pos / float(ROWS) + t1 * col_pos / float(cols * 32 * OWN))
        cos, sin = jnp.cos(angle), jnp.sin(angle)
        incident = []
        for g in range(OWN):
            incident += [cos[32 * g : 32 * g + 32], sin[32 * g : 32 * g + 32]]
        get_screen(0, False)
        start = cmul(screen_on(0, 0), jnp.concatenate(incident, axis=0))
        entering[0] = start
        spread[0, pl.ds(side, own_rows)] = row_step(start)

        def forward_round(k, carry):
            forward(k, False)
            return carry

        def backward_round(k, carry):
            backward(k, False)
            return carry

        if rounds > 1:
            lax.fori_loop(0, rounds - 1, forward_round, 0)
        forward(jnp.int32(rounds - 1), True)
        halo_start(rounds)
        leave_start(jnp.int32(slices - 1))
        wave_turn(leaving.at[home])
        if rounds > 1:
            lax.fori_loop(rounds, 2 * rounds - 1, backward_round, 0)
        backward(jnp.int32(2 * rounds - 1), True)
        grad_turn(grads.at[home])

    @pl.when(porter)
    def _():
        @pl.loop(0, slices)
        def _(j):
            @pl.when(j != home)
            def _():
                leave_copy(j).wait_recv()
                leave_carry(j).start()

        @pl.loop(0, slices)
        def _(i):
            j = slices - 1 - i

            @pl.when(j != home)
            def _():
                grads_copy(j).wait_recv()
                grads_carry(j).start()

    @pl.when(away)
    def _():
        arrived(wave_in, wave_r)
        wave_turn(wave_in)
        arrived(grad_in, gin_r)
        grad_turn(grad_in)

    for t in range(2):
        arrived(waves.at[t, 0], wout_r.at[t])
    for t in range(2):
        arrived(grad_tiles.at[t], gout_r.at[t])
    grad[0] = grad_tiles[0] + grad_tiles[1]

    for t, d, wanted, device in tile_hubs():
        pl.when(wanted)(
            functools.partial(sent, phase.at[0], tiles_in.at[d, row], tile_s.at[t, d], tile_r.at[d], device)
        )

    @pl.when(z == home)
    def _():
        for t in range(2):
            sent(*level_args(t))

    @pl.when(hub)
    def _():
        for r in range(4):
            sent(*wave_args(r))
            sent(*grad_args(r))
        pl.when(wide)(lambda: sent(*wide_args()))
        pl.when(jnp.logical_not(wide))(lambda: sent(*own_args()))

    @pl.when(worker)
    def _():
        @pl.loop(0, 2 * rounds)
        def _(k):
            halo_sent(k)

    @pl.when(z == home)
    def _():
        @pl.loop(0, slices)
        def _(j):
            @pl.when(j != home)
            def _():
                leave_copy(j).wait_send()
                grads_copy(j).wait_send()


def solution(mesh):
    depth, cols = mesh.shape["depth"], mesh.shape["col"]
    y_lo = 4 if cols % 8 == 0 else 1
    slices = depth
    rounds = 2 * slices // RUN
    reach = OWN + 2 * (RUN - 1)
    constants = [jnp.asarray(m) for m in matrices()]

    def body(phase, tilt, intensity):
        hbm = pl.BlockSpec(memory_space=pltpu.HBM)
        vmem = pl.BlockSpec(memory_space=pltpu.VMEM)
        dma = pltpu.SemaphoreType.DMA
        strip = (64 * OWN, ROWS)
        flops = 2 * 2 * slices * 64 * 7 * ROWS * (3 * 512 + 3 * 256)
        return pl.pallas_call(
            functools.partial(kernel, depth, cols, y_lo, slices),
            out_shape=(
                jax.ShapeDtypeStruct((1, 64, 128), F32),
                jax.ShapeDtypeStruct((2, 1, 2, 64, 128), F32),
            ),
            in_specs=[hbm] * 6,
            out_specs=(vmem, vmem),
            scratch_shapes=[
                pltpu.VMEM((1, 64, 128), F32),
                pltpu.SMEM((2, 2), jnp.int32),
                pltpu.VMEM((2, 64, 128), F32),
                pltpu.VMEM((ROWS, 2 * ROWS), BF16),
                pltpu.VMEM((ROWS, 2 * ROWS), BF16),
                pltpu.VMEM((256, 256), BF16),
                pltpu.VMEM((3, 4, 64, 128), F32),
                pltpu.VMEM((4, 64, 128), F32),
                pltpu.VMEM((32 * reach, ROWS), F32),
                pltpu.VMEM((slices, 32 * reach, ROWS), F32),
                pltpu.VMEM((slices, 64 * reach, ROWS), F32),
                pltpu.VMEM((slices,) + strip, F32),
                pltpu.VMEM((slices,) + strip, F32),
                pltpu.VMEM((rounds, 64 * (OWN + 2 * RUN), ROWS), F32),
                pltpu.VMEM((64 * reach, ROWS), F32),
                pltpu.VMEM((slices, 32 * OWN, ROWS), F32),
                pltpu.VMEM(strip, F32),
                pltpu.VMEM((32 * OWN, ROWS), F32),
                pltpu.VMEM((4, 2, 64, 128), F32),
                pltpu.VMEM((4, 64, 128), F32),
                pltpu.VMEM((2, 64, 128), F32),
                dma((6,)),
                dma((2, 3)),
                dma((3,)),
                dma((2,)),
                dma,
                dma,
                dma((slices,)),
                dma((2, rounds)),
                dma((2, rounds)),
                dma((slices,)),
                dma((slices,)),
                dma,
                dma((slices,)),
                dma((slices,)),
                dma,
                dma((4,)),
                dma((2,)),
                dma((4,)),
                dma((2,)),
            ],
            compiler_params=pltpu.CompilerParams(
                collective_id=0, has_side_effects=True, vmem_limit_bytes=36 * 2**20
            ),
            cost_estimate=pl.CostEstimate(flops=flops, bytes_accessed=2**21, transcendentals=2**18),
        )(phase, tilt, intensity, *constants)

    placed = (P("depth", "row", "col"), P(), P(None, "row", "col"))
    return jax.shard_map(
        body,
        mesh=mesh,
        in_specs=placed,
        out_specs=(P("depth", "row", "col"), P(None, "depth", None, "row", "col")),
        check_vma=False,
    )
```

```python
import functools
import math

import jax
import jax.numpy as jnp
import numpy as np
from jax import lax
from jax.experimental import pallas as pl
from jax.experimental.pallas import tpu as pltpu
from jax.sharding import PartitionSpec as P

HALO = 32
FRESNEL = 64
WIDTH = 32
OWN = 4
RUN = 4
ROWS = 256
HOME = 2
MESH = pl.DeviceIdType.MESH
F32 = jnp.float32
BF16 = jnp.bfloat16


def taps(offset):
    offset = offset.astype(np.float64)
    dist = np.maximum(np.abs(offset) - 0.5 * HALO, 0.0)
    profile = np.cos(np.pi * dist / (HALO + 2.0))
    weight = profile * profile / math.sqrt(FRESNEL)
    angle = np.pi * offset * offset / FRESNEL
    inside = np.abs(offset) <= HALO
    re = np.where(inside, np.cos(angle) * weight, 0.0).astype(np.float32)
    im = np.where(inside, np.sin(angle) * weight, 0.0).astype(np.float32)
    return re, im


def halves(matrix):
    high = matrix.astype(BF16)
    low = (matrix - high.astype(np.float32)).astype(BF16)
    return high, low


def matrices():
    i = np.arange(ROWS)
    re, im = taps(i[None, :] - i[:, None])
    row_high, row_low = halves(np.concatenate([re, im], axis=1))

    lines = []
    for o in range(2):
        out = WIDTH * o + np.arange(WIDTH)
        top, low = [], []
        for i in range(4):
            re, im = taps(out[:, None] - (WIDTH * (i - 1) + np.arange(WIDTH))[None, :])
            top += [re, -im]
            low += [im, re]
        lines += [np.concatenate(top, 1), np.concatenate(low, 1)]
    pair = np.concatenate(halves(np.concatenate(lines, 0)), 0)
    return row_high, row_low, pair


def split(value):
    high = value.astype(BF16)
    return high, (value - high.astype(F32)).astype(BF16)


def dot(a, b):
    return jnp.dot(a, b, preferred_element_type=F32)


def blocks_of(value):
    for g in range(value.shape[0] // 64):
        yield value[64 * g : 64 * g + 32], value[64 * g + 32 : 64 * g + 64]


def cmul(a, b):
    out = []
    for (ar, ai), (br, bi) in zip(blocks_of(a), blocks_of(b)):
        out += [ar * br - ai * bi, ar * bi + ai * br]
    return jnp.concatenate(out, axis=0)


def cos_sin(x):
    y = x * x
    c = F32(-1.0 / math.factorial(14))
    s = F32(-1.0 / math.factorial(15))
    for n in range(6, -1, -1):
        sign = -1.0 if n % 2 else 1.0
        c = c * y + F32(sign / math.factorial(2 * n))
        s = s * y + F32(sign / math.factorial(2 * n + 1))
    return c, s * x


def kernel(
    depth, cols, y_lo, slices,
    phase_h, tilt_h, intensity_h, row_high_h, row_low_h, pair_h,
    grad, waves,
    phase, tilt, intensity, row_high, row_low, pair,
    tiles_in, levels_in, strip_out, phase_w, screens, entering, leaving, spread, work, grads,
    wave_in, grad_in, wave_out, grad_out, grad_tiles,
    load_s, tile_s, tile_r, level_s, level_r, strip_s, strip_r, halo_s, halo_r, leave_s, leave_r, wave_r,
    grads_s, grads_r, gin_r, wout_s, wout_r, gout_s, gout_r,
):
    z, row, col = lax.axis_index("depth"), lax.axis_index("row"), lax.axis_index("col")
    ring = 2 * y_lo
    half = cols // ring
    rounds = slices // RUN
    rim = RUN - 1
    own_rows = 64 * OWN
    side = 64 * RUN

    loads = [
        pltpu.make_async_copy(src, dst, load_s.at[i])
        for i, (src, dst) in enumerate(
            (
                (phase_h, phase), (intensity_h, intensity), (tilt_h, tilt),
                (row_high_h, row_high), (row_low_h, row_low), (pair_h, pair),
            )
        )
    ]
    for load in loads:
        load.start()

    x = col // y_lo
    y = (row // 2) * y_lo + col % y_lo
    b = x // half
    place_x = x % half
    strip = place_x * ring + y + (place_x % 2) * (ring - 1 - 2 * y)
    hub = row % 2 == 0
    home = min(HOME, depth - 1)
    worker = hub & (z == home)
    porter = jnp.logical_not(hub) & (z == home)
    base_row = row - row % 2
    wide = z % RUN != 0

    def hub_place(tilt_index, s):
        sx = s // ring
        turn = s % ring
        hy = turn + (sx % 2) * (ring - 1 - 2 * turn)
        return (hy // y_lo) * 2, (tilt_index * half + sx) * y_lo + hy % y_lo

    def clamp(s):
        return jnp.minimum(jnp.maximum(s, 0), cols - 1)

    left = (z,) + hub_place(b, clamp(strip - 1))
    right = (z,) + hub_place(b, clamp(strip + 1))
    has_left = worker & (strip > 0)
    has_right = worker & (strip < cols - 1)

    def same(device):
        return (device[0] == z) & (device[1] == row) & (device[2] == col)

    def remote(src, dst, send, recv, device):
        return pltpu.make_async_remote_copy(
            src_ref=src, dst_ref=dst, send_sem=send, recv_sem=recv, device_id=device, device_id_type=MESH
        )

    def push(src, dst, send, recv, device):
        me = same(device)

        @pl.when(jnp.logical_not(me))
        def _():
            remote(src, dst, send, recv, device).start()

        @pl.when(me)
        def _():
            pltpu.make_async_copy(src, dst, recv).start()

    def sent(src, dst, send, recv, device):
        @pl.when(jnp.logical_not(same(device)))
        def _():
            remote(src, dst, send, recv, device).wait_send()

    def arrived(buffer, recv):
        pltpu.make_async_copy(buffer, buffer, recv).wait()

    def tile_args(t):
        return phase.at[0], tiles_in.at[row], tile_s.at[t], tile_r, (z,) + hub_place(t, col)

    def strip_args(side_of):
        s = strip + side_of
        device = (jnp.int32(home),) + hub_place(b, clamp(s))
        if side_of == 0:
            src, at, size = 0, 32 * rim, 32 * OWN
        elif side_of < 0:
            src, at, size = 0, 32 * (rim + OWN), 32 * rim
        else:
            src, at, size = 32 * (OWN - rim), 0, 32 * rim
        return (
            strip_out.at[pl.ds(src, size)], phase_w.at[z, pl.ds(at, size)],
            strip_s.at[side_of + 1], strip_r.at[1 - side_of, z], device,
        )

    def strip_wanted(side_of):
        if side_of == 0:
            return hub
        return hub & wide & (strip + side_of >= 0) & (strip + side_of < cols)

    barrier = pltpu.get_barrier_semaphore()

    def greet(condition, device):
        @pl.when(condition)
        def _():
            pl.semaphore_signal(barrier, inc=1, device_id=device, device_id_type=MESH)

        return condition.astype(jnp.int32)

    expected = jnp.int32(0)
    for t in range(2):
        device = (z,) + hub_place(t, col)
        expected += greet(jnp.logical_not(same(device)), device)
    for r in range(4):
        device = (z, jnp.int32(r), strip)
        expected += greet(hub & jnp.logical_not(same(device)), device)
    away = hub & (z != home)
    for plane in range(depth):
        if plane != home:
            greet(worker, (jnp.int32(plane), row, col))
            if plane % RUN != 0:
                greet(has_left, (jnp.int32(plane),) + left[1:])
                greet(has_right, (jnp.int32(plane),) + right[1:])
    for side_of in (-1, 0, 1):
        expected += (strip_wanted(side_of) & (z != home)).astype(jnp.int32)
    greet(away, (jnp.int32(home), row + 1, col))
    greet(porter, (z, base_row, col))
    early = away & (z < home)
    greet(early, (jnp.int32(home), row, col))
    expected += worker.astype(jnp.int32) * (1 + home) + porter.astype(jnp.int32) * (depth - 1)
    expected += greet(has_left, left)
    expected += greet(has_right, right)

    loads[0].wait()
    loads[1].wait()
    pl.semaphore_wait(barrier, expected)

    for t in range(2):
        push(*tile_args(t))

    def level_args(t):
        return intensity.at[t], levels_in.at[row], level_s.at[t], level_r, (z,) + hub_place(t, col)

    @pl.when(z == home)
    def _():
        for t in range(2):
            push(*level_args(t))

    def turn_tiles(tiles, h):
        return jnp.concatenate([tiles[2 * h], tiles[2 * h + 1]], axis=0).T

    @pl.when(hub)
    def _():
        arrived(tiles_in, tile_r)
        for h in range(2):
            strip_out[:, 128 * h : 128 * h + 128] = turn_tiles(tiles_in, h)
        for side_of in (0, -1, 1):
            pl.when(strip_wanted(side_of))(functools.partial(push, *strip_args(side_of)))

    for load in loads[2:]:
        load.wait()

    def row_step(value):
        high, low = split(value)
        full = dot(high, row_high[...]) + (dot(low, row_high[...]) + dot(high, row_low[...]))
        out = []
        for a, c in blocks_of(full):
            out += [a[:, :ROWS] - c[:, ROWS:], c[:, :ROWS] + a[:, ROWS:]]
        return jnp.concatenate(out, axis=0)

    def col_step(value):
        high, low = split(value)
        out = []
        for p in range(value.shape[0] // 128 - 1):
            h, l = high[128 * p : 128 * p + 256], low[128 * p : 128 * p + 256]
            both = dot(pair[...], h)
            out.append(both[:128] + (both[128:] + dot(pair[:128], l)))
        return jnp.concatenate(out, axis=0)

    def halo_copies(k):
        return (
            remote(
                spread.at[k, pl.ds(side, side)], spread.at[k, pl.ds(side + own_rows, side)],
                halo_s.at[0, k], halo_r.at[1, k], left,
            ),
            remote(
                spread.at[k, pl.ds(own_rows, side)], spread.at[k, pl.ds(0, side)],
                halo_s.at[1, k], halo_r.at[0, k], right,
            ),
        )

    def halo_start(k):
        to_left, to_right = halo_copies(k)
        pl.when(has_left)(to_left.start)
        pl.when(has_right)(to_right.start)

    def halo_wait(k):
        to_left, to_right = halo_copies(k)
        pl.when(has_left)(to_right.wait_recv)
        pl.when(has_right)(to_left.wait_recv)

    def halo_sent(k):
        to_left, to_right = halo_copies(k)
        pl.when(has_left)(to_left.wait_send)
        pl.when(has_right)(to_right.wait_send)

    def make_screen(j, with_rim):
        for g in range(0 if with_rim else rim, OWN + (2 * rim if with_rim else rim)):
            c, s = cos_sin(phase_w[j, 32 * g : 32 * g + 32])
            if g < rim:
                c, s = jnp.where(strip > 0, c, 0.0), jnp.where(strip > 0, s, 0.0)
            if g >= rim + OWN:
                c, s = jnp.where(strip < cols - 1, c, 0.0), jnp.where(strip < cols - 1, s, 0.0)
            screens[j, 64 * g : 64 * g + 32] = c
            screens[j, 64 * g + 32 : 64 * g + 64] = s

    def get_screen(j, with_rim):
        span = pl.ds(32 * rim, 32 * OWN)
        arrived(phase_w.at[j, span], strip_r.at[1, j])
        if with_rim:
            low, high = pl.ds(0, 32 * rim), pl.ds(32 * (rim + OWN), 32 * rim)
            pl.when(strip > 0)(lambda: arrived(phase_w.at[j, low], strip_r.at[0, j]))
            pl.when(strip < cols - 1)(lambda: arrived(phase_w.at[j, high], strip_r.at[2, j]))
        make_screen(j, with_rim)

    def screen_on(j, out):
        return screens[j, pl.ds(64 * (rim - out), 64 * (OWN + 2 * out))]

    def leave_copy(j):
        return remote(leaving.at[j], leaving.at[j], leave_s.at[j], leave_r.at[j], (z, base_row + 1, col))

    def grads_copy(j):
        return remote(grads.at[j], grads.at[j], grads_s.at[j], grads_r.at[j], (z, base_row + 1, col))

    def leave_carry(j):
        return remote(leaving.at[j], wave_in, leave_s.at[j], wave_r, (j, base_row, col))

    def grads_carry(j):
        return remote(grads.at[j], grad_in, grads_s.at[j], gin_r, (j, base_row, col))

    def leave_start(j):
        pl.when(j != home)(leave_copy(j).start)

    def grads_start(j):
        pl.when(j > home)(grads_copy(j).start)
        pl.when(j < home)(grads_carry(j).start)

    def wave_turn(src):
        for c in range(2):
            value = jnp.concatenate([src[64 * g + 32 * c : 64 * g + 32 * c + 32] for g in range(OWN)], axis=0)
            for h in range(2):
                turned = value[:, 128 * h : 128 * h + 128].T
                wave_out[2 * h, c] = turned[:64]
                wave_out[2 * h + 1, c] = turned[64:]
        for r in range(4):
            push(*wave_args(r))

    def wave_args(r):
        return wave_out.at[r], waves.at[b, 0], wout_s.at[r], wout_r.at[b], (z, jnp.int32(r), strip)

    def grad_turn(src):
        for h in range(2):
            turned = src[:, 128 * h : 128 * h + 128].T
            grad_out[2 * h] = turned[:64]
            grad_out[2 * h + 1] = turned[64:]
        for r in range(4):
            push(*grad_args(r))

    def grad_args(r):
        return grad_out.at[r], grad_tiles.at[b], gout_s.at[r], gout_r.at[b], (z, jnp.int32(r), strip)

    def next_input(i, k):
        return spread[k] if i == 1 else work[pl.ds(0, 64 * (OWN + 2 * (RUN - i + 1)))]

    def own_part(value, out):
        return value[64 * out : 64 * out + own_rows]

    def forward(k, last):
        first_slice = k * RUN
        halo_start(k)
        pl.when(k > 0)(lambda: leave_start(first_slice - 1))
        for i in range(1, RUN):
            get_screen(first_slice + i, True)
        halo_wait(k)
        for i in range(1, RUN + 1):
            out = RUN - i
            j = first_slice + i - 1
            wave = col_step(next_input(i, k))
            leaving[j] = own_part(wave, out)
            if i < RUN:
                leave_start(j)
            elif not last:
                get_screen(j + 1, False)
            if i < RUN:
                after = cmul(screen_on(j + 1, out), wave)
                entering[j + 1] = own_part(after, out)
                work[pl.ds(0, 64 * (OWN + 2 * out))] = row_step(after)
            elif not last:
                after = cmul(screen_on(j + 1, 0), wave)
                entering[j + 1] = after
                spread[k + 1, pl.ds(side, own_rows)] = row_step(after)
            else:
                arrived(levels_in, level_r)
                level = jnp.concatenate([turn_tiles(levels_in, h) for h in range(2)], axis=1)
                seed = []
                for g, (re, im) in enumerate(blocks_of(wave)):
                    misfit = 2.0 * (re * re + im * im - level[32 * g : 32 * g + 32])
                    seed += [misfit * re, -(misfit * im)]
                spread[k + 1, pl.ds(side, own_rows)] = row_step(jnp.concatenate(seed, axis=0))

    def backward(k, last):
        first_slice = (2 * rounds - k) * RUN - 1
        halo_wait(k)
        for i in range(1, RUN + 1):
            out = RUN - i
            j = first_slice - (i - 1)
            pulled = col_step(next_input(i, k))
            if i < RUN:
                work[pl.ds(0, 64 * (OWN + 2 * out))] = row_step(cmul(screen_on(j, out), pulled))
            elif not last:
                spread[k + 1, pl.ds(side, own_rows)] = row_step(cmul(screen_on(j, 0), pulled))
                halo_start(k + 1)
            parts = []
            for (pr, pi), (er, ei) in zip(blocks_of(own_part(pulled, out)), blocks_of(entering[j])):
                parts.append(-(pr * ei + pi * er))
            grads[j] = jnp.concatenate(parts, axis=0)
            grads_start(j)

    @pl.when(worker)
    def _():
        @pl.when(strip == 0)
        def _():
            @pl.loop(0, 2 * rounds)
            def _(k):
                spread[k, pl.ds(0, side)] = jnp.zeros((side, ROWS), F32)

            @pl.loop(0, slices)
            def _(j):
                phase_w[j, pl.ds(0, 32 * rim)] = jnp.zeros((32 * rim, ROWS), F32)

        @pl.when(strip == cols - 1)
        def _():
            @pl.loop(0, 2 * rounds)
            def _(k):
                spread[k, pl.ds(side + own_rows, side)] = jnp.zeros((side, ROWS), F32)

            @pl.loop(0, slices)
            def _(j):
                phase_w[j, pl.ds(32 * (rim + OWN), 32 * rim)] = jnp.zeros((32 * rim, ROWS), F32)

        row_pos = lax.broadcasted_iota(jnp.int32, (32 * OWN, ROWS), 1).astype(F32)
        col_pos = (strip * (32 * OWN) + lax.broadcasted_iota(jnp.int32, (32 * OWN, ROWS), 0)).astype(F32)
        t0, t1 = tilt[b, 0].astype(F32), tilt[b, 1].astype(F32)
        angle = 2.0 * jnp.pi * (t0 * row_pos / float(ROWS) + t1 * col_pos / float(cols * 32 * OWN))
        cos, sin = jnp.cos(angle), jnp.sin(angle)
        incident = []
        for g in range(OWN):
            incident += [cos[32 * g : 32 * g + 32], sin[32 * g : 32 * g + 32]]
        get_screen(0, False)
        start = cmul(screen_on(0, 0), jnp.concatenate(incident, axis=0))
        entering[0] = start
        spread[0, pl.ds(side, own_rows)] = row_step(start)

        def forward_round(k, carry):
            forward(k, False)
            return carry

        def backward_round(k, carry):
            backward(k, False)
            return carry

        if rounds > 1:
            lax.fori_loop(0, rounds - 1, forward_round, 0)
        forward(jnp.int32(rounds - 1), True)
        halo_start(rounds)
        leave_start(jnp.int32(slices - 1))
        wave_turn(leaving.at[home])
        if rounds > 1:
            lax.fori_loop(rounds, 2 * rounds - 1, backward_round, 0)
        backward(jnp.int32(2 * rounds - 1), True)
        grad_turn(grads.at[home])

    @pl.when(porter)
    def _():
        @pl.loop(0, slices)
        def _(j):
            @pl.when(j != home)
            def _():
                leave_copy(j).wait_recv()
                leave_carry(j).start()

        @pl.loop(0, slices)
        def _(i):
            j = slices - 1 - i

            @pl.when(j > home)
            def _():
                grads_copy(j).wait_recv()
                grads_carry(j).start()

    @pl.when(away)
    def _():
        arrived(wave_in, wave_r)
        wave_turn(wave_in)
        arrived(grad_in, gin_r)
        grad_turn(grad_in)

    for t in range(2):
        arrived(waves.at[t, 0], wout_r.at[t])
    for t in range(2):
        arrived(grad_tiles.at[t], gout_r.at[t])
    grad[0] = grad_tiles[0] + grad_tiles[1]

    for t in range(2):
        sent(*tile_args(t))

    @pl.when(z == home)
    def _():
        for t in range(2):
            sent(*level_args(t))

    @pl.when(hub)
    def _():
        for r in range(4):
            sent(*wave_args(r))
            sent(*grad_args(r))
        for side_of in (-1, 0, 1):
            pl.when(strip_wanted(side_of))(functools.partial(sent, *strip_args(side_of)))

    @pl.when(worker)
    def _():
        @pl.loop(0, 2 * rounds)
        def _(k):
            halo_sent(k)

    @pl.when(z == home)
    def _():
        @pl.loop(0, slices)
        def _(j):
            @pl.when(j != home)
            def _():
                leave_copy(j).wait_send()
                pl.when(hub | (j > home))(grads_copy(j).wait_send)


def solution(mesh):
    depth, cols = mesh.shape["depth"], mesh.shape["col"]
    y_lo = 4 if cols % 8 == 0 else 1
    slices = depth
    rounds = 2 * slices // RUN
    reach = OWN + 2 * (RUN - 1)
    constants = [jnp.asarray(m) for m in matrices()]

    def body(phase, tilt, intensity):
        hbm = pl.BlockSpec(memory_space=pltpu.HBM)
        vmem = pl.BlockSpec(memory_space=pltpu.VMEM)
        dma = pltpu.SemaphoreType.DMA
        strip = (64 * OWN, ROWS)
        flops = 2 * 2 * slices * 64 * 7 * ROWS * (3 * 512 + 3 * 256)
        return pl.pallas_call(
            functools.partial(kernel, depth, cols, y_lo, slices),
            out_shape=(
                jax.ShapeDtypeStruct((1, 64, 128), F32),
                jax.ShapeDtypeStruct((2, 1, 2, 64, 128), F32),
            ),
            in_specs=[hbm] * 6,
            out_specs=(vmem, vmem),
            scratch_shapes=[
                pltpu.VMEM((1, 64, 128), F32),
                pltpu.SMEM((2, 2), jnp.int32),
                pltpu.VMEM((2, 64, 128), F32),
                pltpu.VMEM((ROWS, 2 * ROWS), BF16),
                pltpu.VMEM((ROWS, 2 * ROWS), BF16),
                pltpu.VMEM((256, 256), BF16),
                pltpu.VMEM((4, 64, 128), F32),
                pltpu.VMEM((4, 64, 128), F32),
                pltpu.VMEM((32 * OWN, ROWS), F32),
                pltpu.VMEM((slices, 32 * reach, ROWS), F32),
                pltpu.VMEM((slices, 64 * reach, ROWS), F32),
                pltpu.VMEM((slices,) + strip, F32),
                pltpu.VMEM((slices,) + strip, F32),
                pltpu.VMEM((rounds, 64 * (OWN + 2 * RUN), ROWS), F32),
                pltpu.VMEM((64 * reach, ROWS), F32),
                pltpu.VMEM((slices, 32 * OWN, ROWS), F32),
                pltpu.VMEM(strip, F32),
                pltpu.VMEM((32 * OWN, ROWS), F32),
                pltpu.VMEM((4, 2, 64, 128), F32),
                pltpu.VMEM((4, 64, 128), F32),
                pltpu.VMEM((2, 64, 128), F32),
                dma((6,)),
                dma((2,)),
                dma,
                dma((2,)),
                dma,
                dma((3,)),
                dma((3, slices)),
                dma((2, rounds)),
                dma((2, rounds)),
                dma((slices,)),
                dma((slices,)),
                dma,
                dma((slices,)),
                dma((slices,)),
                dma,
                dma((4,)),
                dma((2,)),
                dma((4,)),
                dma((2,)),
            ],
            compiler_params=pltpu.CompilerParams(
                collective_id=0, has_side_effects=True, vmem_limit_bytes=56 * 2**20
            ),
            cost_estimate=pl.CostEstimate(flops=flops, bytes_accessed=2**21, transcendentals=2**18),
        )(phase, tilt, intensity, *constants)

    placed = (P("depth", "row", "col"), P(), P(None, "row", "col"))
    return jax.shard_map(
        body,
        mesh=mesh,
        in_specs=placed,
        out_specs=(P("depth", "row", "col"), P(None, "depth", None, "row", "col")),
        check_vma=False,
    )
```

```python
import functools
import math

import jax
import jax.numpy as jnp
import numpy as np
from jax import lax
from jax.experimental import pallas as pl
from jax.experimental.pallas import tpu as pltpu
from jax.sharding import PartitionSpec as P

HALO = 32
FRESNEL = 64
WIDTH = 32
OWN = 4
RUN = 4
ROWS = 256
HOME = 1
MESH = pl.DeviceIdType.MESH
F32 = jnp.float32
BF16 = jnp.bfloat16


def taps(offset):
    offset = offset.astype(np.float64)
    dist = np.maximum(np.abs(offset) - 0.5 * HALO, 0.0)
    profile = np.cos(np.pi * dist / (HALO + 2.0))
    weight = profile * profile / math.sqrt(FRESNEL)
    angle = np.pi * offset * offset / FRESNEL
    inside = np.abs(offset) <= HALO
    re = np.where(inside, np.cos(angle) * weight, 0.0).astype(np.float32)
    im = np.where(inside, np.sin(angle) * weight, 0.0).astype(np.float32)
    return re, im


def halves(matrix):
    high = matrix.astype(BF16)
    low = (matrix - high.astype(np.float32)).astype(BF16)
    return high, low


def matrices():
    i = np.arange(ROWS)
    re, im = taps(i[None, :] - i[:, None])
    row_high, row_low = halves(np.concatenate([re, im], axis=1))

    lines = []
    for o in range(2):
        out = WIDTH * o + np.arange(WIDTH)
        top, low = [], []
        for i in range(4):
            re, im = taps(out[:, None] - (WIDTH * (i - 1) + np.arange(WIDTH))[None, :])
            top += [re, -im]
            low += [im, re]
        lines += [np.concatenate(top, 1), np.concatenate(low, 1)]
    pair = np.concatenate(halves(np.concatenate(lines, 0)), 0)
    return row_high, row_low, pair


def split(value):
    high = value.astype(BF16)
    return high, (value - high.astype(F32)).astype(BF16)


def dot(a, b):
    return jnp.dot(a, b, preferred_element_type=F32)


def blocks_of(value):
    for g in range(value.shape[0] // 64):
        yield value[64 * g : 64 * g + 32], value[64 * g + 32 : 64 * g + 64]


def cmul(a, b):
    out = []
    for (ar, ai), (br, bi) in zip(blocks_of(a), blocks_of(b)):
        out += [ar * br - ai * bi, ar * bi + ai * br]
    return jnp.concatenate(out, axis=0)


def cos_sin(x):
    y = x * x
    c = F32(-1.0 / math.factorial(14))
    s = F32(-1.0 / math.factorial(15))
    for n in range(6, -1, -1):
        sign = -1.0 if n % 2 else 1.0
        c = c * y + F32(sign / math.factorial(2 * n))
        s = s * y + F32(sign / math.factorial(2 * n + 1))
    return c, s * x


def kernel(
    depth, cols, y_lo, slices,
    phase_h, tilt_h, intensity_h, row_high_h, row_low_h, pair_h,
    grad, waves,
    phase, tilt, intensity, row_high, row_low, pair,
    tiles_in, levels_in, strip_out, phase_w, screens, entering, leaving, spread, work, grads,
    wave_in, grad_in, wave_out, grad_out, grad_tiles,
    load_s, tile_s, tile_r, level_s, level_r, strip_s, strip_r, halo_s, halo_r, leave_s, leave_r, wave_r,
    grads_s, grads_r, gin_r, wout_s, wout_r, gout_s, gout_r, ready,
):
    z, row, col = lax.axis_index("depth"), lax.axis_index("row"), lax.axis_index("col")
    ring = 2 * y_lo
    half = cols // ring
    rounds = slices // RUN
    rim = RUN - 1
    own_rows = 64 * OWN
    side = 64 * RUN

    loads = [
        pltpu.make_async_copy(src, dst, load_s.at[i])
        for i, (src, dst) in enumerate(
            (
                (phase_h, phase), (intensity_h, intensity), (tilt_h, tilt),
                (row_high_h, row_high), (row_low_h, row_low), (pair_h, pair),
            )
        )
    ]
    for load in loads:
        load.start()

    x = col // y_lo
    y = (row // 2) * y_lo + col % y_lo
    b = x // half
    place_x = x % half
    strip = place_x * ring + y + (place_x % 2) * (ring - 1 - 2 * y)
    hub = row % 2 == 0
    home = min(HOME, depth - 1)
    worker = hub & (z == home)
    porter = jnp.logical_not(hub) & (z == home)
    base_row = row - row % 2
    wide = z % RUN != 0

    def hub_place(tilt_index, s):
        sx = s // ring
        turn = s % ring
        hy = turn + (sx % 2) * (ring - 1 - 2 * turn)
        return (hy // y_lo) * 2, (tilt_index * half + sx) * y_lo + hy % y_lo

    def clamp(s):
        return jnp.minimum(jnp.maximum(s, 0), cols - 1)

    left = (z,) + hub_place(b, clamp(strip - 1))
    right = (z,) + hub_place(b, clamp(strip + 1))
    has_left = worker & (strip > 0)
    has_right = worker & (strip < cols - 1)

    def same(device):
        return (device[0] == z) & (device[1] == row) & (device[2] == col)

    def remote(src, dst, send, recv, device):
        return pltpu.make_async_remote_copy(
            src_ref=src, dst_ref=dst, send_sem=send, recv_sem=recv, device_id=device, device_id_type=MESH
        )

    def push(src, dst, send, recv, device):
        me = same(device)

        @pl.when(jnp.logical_not(me))
        def _():
            remote(src, dst, send, recv, device).start()

        @pl.when(me)
        def _():
            pltpu.make_async_copy(src, dst, recv).start()

    def sent(src, dst, send, recv, device):
        @pl.when(jnp.logical_not(same(device)))
        def _():
            remote(src, dst, send, recv, device).wait_send()

    def arrived(buffer, recv):
        pltpu.make_async_copy(buffer, buffer, recv).wait()

    def tile_args(t):
        return phase.at[0], tiles_in.at[row], tile_s.at[t], tile_r, (z,) + hub_place(t, col)

    def strip_args(side_of):
        s = strip + side_of
        device = (jnp.int32(home),) + hub_place(b, clamp(s))
        if side_of == 0:
            src, at, size = 0, 32 * rim, 32 * OWN
        elif side_of < 0:
            src, at, size = 0, 32 * (rim + OWN), 32 * rim
        else:
            src, at, size = 32 * (OWN - rim), 0, 32 * rim
        return (
            strip_out.at[pl.ds(src, size)], phase_w.at[z, pl.ds(at, size)],
            strip_s.at[side_of + 1], strip_r.at[1 - side_of, z], device,
        )

    def strip_wanted(side_of):
        if side_of == 0:
            return hub
        return hub & wide & (strip + side_of >= 0) & (strip + side_of < cols)

    barrier = pltpu.get_barrier_semaphore()

    def greet(condition, device):
        @pl.when(condition)
        def _():
            pl.semaphore_signal(barrier, inc=1, device_id=device, device_id_type=MESH)

        return condition.astype(jnp.int32)

    expected = jnp.int32(0)
    for t in range(2):
        device = (z,) + hub_place(t, col)
        expected += greet(jnp.logical_not(same(device)), device)
    for r in range(4):
        device = (z, jnp.int32(r), strip)
        expected += greet(hub & jnp.logical_not(same(device)), device)
    away = hub & (z != home)
    for plane in range(depth):
        if plane != home:
            greet(worker, (jnp.int32(plane), row, col))
            if plane % RUN != 0:
                greet(has_left, (jnp.int32(plane),) + left[1:])
                greet(has_right, (jnp.int32(plane),) + right[1:])
            for r in range(4 if plane < home else 0):
                greet(worker, (jnp.int32(plane), jnp.int32(r), strip))
            greet(porter, (jnp.int32(plane), base_row, col))
    for side_of in (-1, 0, 1):
        expected += (strip_wanted(side_of) & (z != home)).astype(jnp.int32)
    greet(porter, (z, base_row, col))
    early = z < home
    expected += away.astype(jnp.int32) + worker.astype(jnp.int32) + 2 * early.astype(jnp.int32)
    expected += greet(has_left, left)
    expected += greet(has_right, right)

    loads[0].wait()
    loads[1].wait()
    pl.semaphore_wait(barrier, expected)

    def ready_signal(condition, device):
        @pl.when(condition)
        def _():
            pl.semaphore_signal(ready, inc=1, device_id=device, device_id_type=MESH)


    for t in range(2):
        push(*tile_args(t))

    ready_signal(away, (jnp.int32(home), row + 1, col))
    for t in range(2):
        ready_signal(early, (jnp.int32(home),) + hub_place(t, col))

    def level_args(t):
        return intensity.at[t], levels_in.at[row], level_s.at[t], level_r, (z,) + hub_place(t, col)

    @pl.when(z == home)
    def _():
        for t in range(2):
            push(*level_args(t))

    def turn_tiles(tiles, h):
        return jnp.concatenate([tiles[2 * h], tiles[2 * h + 1]], axis=0).T

    @pl.when(hub)
    def _():
        arrived(tiles_in, tile_r)
        for h in range(2):
            strip_out[:, 128 * h : 128 * h + 128] = turn_tiles(tiles_in, h)
        for side_of in (0, -1, 1):
            pl.when(strip_wanted(side_of))(functools.partial(push, *strip_args(side_of)))

    for load in loads[2:]:
        load.wait()

    def row_step(value):
        high, low = split(value)
        full = dot(high, row_high[...]) + (dot(low, row_high[...]) + dot(high, row_low[...]))
        out = []
        for a, c in blocks_of(full):
            out += [a[:, :ROWS] - c[:, ROWS:], c[:, :ROWS] + a[:, ROWS:]]
        return jnp.concatenate(out, axis=0)

    def col_step(value):
        high, low = split(value)
        out = []
        for p in range(value.shape[0] // 128 - 1):
            h, l = high[128 * p : 128 * p + 256], low[128 * p : 128 * p + 256]
            both = dot(pair[...], h)
            out.append(both[:128] + (both[128:] + dot(pair[:128], l)))
        return jnp.concatenate(out, axis=0)

    def halo_copies(k):
        return (
            remote(
                spread.at[k, pl.ds(side, side)], spread.at[k, pl.ds(side + own_rows, side)],
                halo_s.at[0, k], halo_r.at[1, k], left,
            ),
            remote(
                spread.at[k, pl.ds(own_rows, side)], spread.at[k, pl.ds(0, side)],
                halo_s.at[1, k], halo_r.at[0, k], right,
            ),
        )

    def halo_start(k):
        to_left, to_right = halo_copies(k)
        pl.when(has_left)(to_left.start)
        pl.when(has_right)(to_right.start)

    def halo_wait(k):
        to_left, to_right = halo_copies(k)
        pl.when(has_left)(to_right.wait_recv)
        pl.when(has_right)(to_left.wait_recv)

    def halo_sent(k):
        to_left, to_right = halo_copies(k)
        pl.when(has_left)(to_left.wait_send)
        pl.when(has_right)(to_right.wait_send)

    def make_screen(j, with_rim):
        for g in range(0 if with_rim else rim, OWN + (2 * rim if with_rim else rim)):
            c, s = cos_sin(phase_w[j, 32 * g : 32 * g + 32])
            if g < rim:
                c, s = jnp.where(strip > 0, c, 0.0), jnp.where(strip > 0, s, 0.0)
            if g >= rim + OWN:
                c, s = jnp.where(strip < cols - 1, c, 0.0), jnp.where(strip < cols - 1, s, 0.0)
            screens[j, 64 * g : 64 * g + 32] = c
            screens[j, 64 * g + 32 : 64 * g + 64] = s

    def get_screen(j, with_rim):
        span = pl.ds(32 * rim, 32 * OWN)
        arrived(phase_w.at[j, span], strip_r.at[1, j])
        if with_rim:
            low, high = pl.ds(0, 32 * rim), pl.ds(32 * (rim + OWN), 32 * rim)
            pl.when(strip > 0)(lambda: arrived(phase_w.at[j, low], strip_r.at[0, j]))
            pl.when(strip < cols - 1)(lambda: arrived(phase_w.at[j, high], strip_r.at[2, j]))
        make_screen(j, with_rim)

    def screen_on(j, out):
        return screens[j, pl.ds(64 * (rim - out), 64 * (OWN + 2 * out))]

    def leave_copy(j):
        return remote(leaving.at[j], leaving.at[j], leave_s.at[j], leave_r.at[j], (z, base_row + 1, col))

    def grads_copy(j):
        return remote(grads.at[j], grads.at[j], grads_s.at[j], grads_r.at[j], (z, base_row + 1, col))

    def leave_carry(j):
        return remote(leaving.at[j], wave_in, leave_s.at[j], wave_r, (j, base_row, col))

    def grads_carry(j):
        return remote(grads.at[j], grad_in, grads_s.at[j], gin_r, (j, base_row, col))

    def leave_start(j):
        pl.when(j != home)(leave_copy(j).start)

    def grads_start(j):
        pl.when(j > home)(grads_copy(j).start)

    def wave_turn(src):
        for c in range(2):
            value = jnp.concatenate([src[64 * g + 32 * c : 64 * g + 32 * c + 32] for g in range(OWN)], axis=0)
            for h in range(2):
                turned = value[:, 128 * h : 128 * h + 128].T
                wave_out[2 * h, c] = turned[:64]
                wave_out[2 * h + 1, c] = turned[64:]
        for r in range(4):
            push(*wave_args(r))

    def wave_args(r):
        return wave_out.at[r], waves.at[b, 0], wout_s.at[r], wout_r.at[b], (z, jnp.int32(r), strip)

    def grad_turn(src, plane, slot):
        for h in range(2):
            turned = src[:, 128 * h : 128 * h + 128].T
            grad_out[slot, 2 * h] = turned[:64]
            grad_out[slot, 2 * h + 1] = turned[64:]
        for r in range(4):
            push(*grad_args(r, plane, slot))

    def grad_args(r, plane, slot):
        device = (plane, jnp.int32(r), strip)
        return grad_out.at[slot, r], grad_tiles.at[b], gout_s.at[slot, r], gout_r.at[b], device

    def next_input(i, k):
        return spread[k] if i == 1 else work[pl.ds(0, 64 * (OWN + 2 * (RUN - i + 1)))]

    def own_part(value, out):
        return value[64 * out : 64 * out + own_rows]

    def forward(k, last):
        first_slice = k * RUN
        halo_start(k)
        pl.when(k > 0)(lambda: leave_start(first_slice - 1))
        for i in range(1, RUN):
            get_screen(first_slice + i, True)
        halo_wait(k)
        for i in range(1, RUN + 1):
            out = RUN - i
            j = first_slice + i - 1
            wave = col_step(next_input(i, k))
            leaving[j] = own_part(wave, out)
            if i < RUN:
                leave_start(j)
            elif not last:
                get_screen(j + 1, False)
            if i < RUN:
                after = cmul(screen_on(j + 1, out), wave)
                entering[j + 1] = own_part(after, out)
                work[pl.ds(0, 64 * (OWN + 2 * out))] = row_step(after)
            elif not last:
                after = cmul(screen_on(j + 1, 0), wave)
                entering[j + 1] = after
                spread[k + 1, pl.ds(side, own_rows)] = row_step(after)
            else:
                arrived(levels_in, level_r)
                level = jnp.concatenate([turn_tiles(levels_in, h) for h in range(2)], axis=1)
                seed = []
                for g, (re, im) in enumerate(blocks_of(wave)):
                    misfit = 2.0 * (re * re + im * im - level[32 * g : 32 * g + 32])
                    seed += [misfit * re, -(misfit * im)]
                spread[k + 1, pl.ds(side, own_rows)] = row_step(jnp.concatenate(seed, axis=0))

    def backward(k, last):
        first_slice = (2 * rounds - k) * RUN - 1
        halo_wait(k)
        for i in range(1, RUN + 1):
            out = RUN - i
            j = first_slice - (i - 1)
            pulled = col_step(next_input(i, k))
            if i < RUN:
                work[pl.ds(0, 64 * (OWN + 2 * out))] = row_step(cmul(screen_on(j, out), pulled))
            elif not last:
                spread[k + 1, pl.ds(side, own_rows)] = row_step(cmul(screen_on(j, 0), pulled))
                halo_start(k + 1)
            parts = []
            for (pr, pi), (er, ei) in zip(blocks_of(own_part(pulled, out)), blocks_of(entering[j])):
                parts.append(-(pr * ei + pi * er))
            grads[j] = jnp.concatenate(parts, axis=0)
            if last and RUN - i <= home:
                plane = RUN - i
                if plane == home - 1:
                    pl.semaphore_wait(ready, 4 * home)
                grad_turn(grads.at[plane], jnp.int32(plane), plane)
            else:
                grads_start(j)

    @pl.when(worker)
    def _():
        @pl.when(strip == 0)
        def _():
            @pl.loop(0, 2 * rounds)
            def _(k):
                spread[k, pl.ds(0, side)] = jnp.zeros((side, ROWS), F32)

            @pl.loop(0, slices)
            def _(j):
                phase_w[j, pl.ds(0, 32 * rim)] = jnp.zeros((32 * rim, ROWS), F32)

        @pl.when(strip == cols - 1)
        def _():
            @pl.loop(0, 2 * rounds)
            def _(k):
                spread[k, pl.ds(side + own_rows, side)] = jnp.zeros((side, ROWS), F32)

            @pl.loop(0, slices)
            def _(j):
                phase_w[j, pl.ds(32 * (rim + OWN), 32 * rim)] = jnp.zeros((32 * rim, ROWS), F32)

        row_pos = lax.broadcasted_iota(jnp.int32, (32 * OWN, ROWS), 1).astype(F32)
        col_pos = (strip * (32 * OWN) + lax.broadcasted_iota(jnp.int32, (32 * OWN, ROWS), 0)).astype(F32)
        t0, t1 = tilt[b, 0].astype(F32), tilt[b, 1].astype(F32)
        angle = 2.0 * jnp.pi * (t0 * row_pos / float(ROWS) + t1 * col_pos / float(cols * 32 * OWN))
        cos, sin = jnp.cos(angle), jnp.sin(angle)
        incident = []
        for g in range(OWN):
            incident += [cos[32 * g : 32 * g + 32], sin[32 * g : 32 * g + 32]]
        get_screen(0, False)
        start = cmul(screen_on(0, 0), jnp.concatenate(incident, axis=0))
        entering[0] = start
        spread[0, pl.ds(side, own_rows)] = row_step(start)

        def forward_round(k, carry):
            forward(k, False)
            return carry

        def backward_round(k, carry):
            backward(k, False)
            return carry

        if rounds > 1:
            lax.fori_loop(0, rounds - 1, forward_round, 0)
        forward(jnp.int32(rounds - 1), True)
        halo_start(rounds)
        leave_start(jnp.int32(slices - 1))
        wave_turn(leaving.at[home])
        if rounds > 1:
            lax.fori_loop(rounds, 2 * rounds - 1, backward_round, 0)
        backward(jnp.int32(2 * rounds - 1), True)

    @pl.when(porter)
    def _():
        pl.semaphore_wait(ready, depth - 1)

        @pl.loop(0, slices)
        def _(j):
            @pl.when(j != home)
            def _():
                leave_copy(j).wait_recv()
                leave_carry(j).start()

        @pl.loop(0, slices)
        def _(i):
            j = slices - 1 - i

            @pl.when(j > home)
            def _():
                grads_copy(j).wait_recv()
                grads_carry(j).start()

    @pl.when(away)
    def _():
        arrived(wave_in, wave_r)
        wave_turn(wave_in)

        @pl.when(z > home)
        def _():
            arrived(grad_in, gin_r)
            grad_turn(grad_in, z, 0)

    for t in range(2):
        arrived(waves.at[t, 0], wout_r.at[t])
    for t in range(2):
        arrived(grad_tiles.at[t], gout_r.at[t])
    grad[0] = grad_tiles[0] + grad_tiles[1]

    for t in range(2):
        sent(*tile_args(t))

    @pl.when(z == home)
    def _():
        for t in range(2):
            sent(*level_args(t))

    @pl.when(hub)
    def _():
        for r in range(4):
            sent(*wave_args(r))
            for plane in range(home + 1):
                pl.when(worker)(functools.partial(sent, *grad_args(r, jnp.int32(plane), plane)))
            pl.when(z > home)(functools.partial(sent, *grad_args(r, z, 0)))
        for side_of in (-1, 0, 1):
            pl.when(strip_wanted(side_of))(functools.partial(sent, *strip_args(side_of)))

    @pl.when(worker)
    def _():
        @pl.loop(0, 2 * rounds)
        def _(k):
            halo_sent(k)

    @pl.when(z == home)
    def _():
        @pl.loop(0, slices)
        def _(j):
            @pl.when(j != home)
            def _():
                leave_copy(j).wait_send()
                pl.when(j > home)(grads_copy(j).wait_send)


def solution(mesh):
    depth, cols = mesh.shape["depth"], mesh.shape["col"]
    y_lo = 4 if cols % 8 == 0 else 1
    slices = depth
    rounds = 2 * slices // RUN
    reach = OWN + 2 * (RUN - 1)
    constants = [jnp.asarray(m) for m in matrices()]

    def body(phase, tilt, intensity):
        hbm = pl.BlockSpec(memory_space=pltpu.HBM)
        vmem = pl.BlockSpec(memory_space=pltpu.VMEM)
        dma = pltpu.SemaphoreType.DMA
        strip = (64 * OWN, ROWS)
        flops = 2 * 2 * slices * 64 * 7 * ROWS * (3 * 512 + 3 * 256)
        return pl.pallas_call(
            functools.partial(kernel, depth, cols, y_lo, slices),
            out_shape=(
                jax.ShapeDtypeStruct((1, 64, 128), F32),
                jax.ShapeDtypeStruct((2, 1, 2, 64, 128), F32),
            ),
            in_specs=[hbm] * 6,
            out_specs=(vmem, vmem),
            scratch_shapes=[
                pltpu.VMEM((1, 64, 128), F32),
                pltpu.SMEM((2, 2), jnp.int32),
                pltpu.VMEM((2, 64, 128), F32),
                pltpu.VMEM((ROWS, 2 * ROWS), BF16),
                pltpu.VMEM((ROWS, 2 * ROWS), BF16),
                pltpu.VMEM((256, 256), BF16),
                pltpu.VMEM((4, 64, 128), F32),
                pltpu.VMEM((4, 64, 128), F32),
                pltpu.VMEM((32 * OWN, ROWS), F32),
                pltpu.VMEM((slices, 32 * reach, ROWS), F32),
                pltpu.VMEM((slices, 64 * reach, ROWS), F32),
                pltpu.VMEM((slices,) + strip, F32),
                pltpu.VMEM((slices,) + strip, F32),
                pltpu.VMEM((rounds, 64 * (OWN + 2 * RUN), ROWS), F32),
                pltpu.VMEM((64 * reach, ROWS), F32),
                pltpu.VMEM((slices, 32 * OWN, ROWS), F32),
                pltpu.VMEM(strip, F32),
                pltpu.VMEM((32 * OWN, ROWS), F32),
                pltpu.VMEM((4, 2, 64, 128), F32),
                pltpu.VMEM((HOME + 1, 4, 64, 128), F32),
                pltpu.VMEM((2, 64, 128), F32),
                dma((6,)),
                dma((2,)),
                dma,
                dma((2,)),
                dma,
                dma((3,)),
                dma((3, slices)),
                dma((2, rounds)),
                dma((2, rounds)),
                dma((slices,)),
                dma((slices,)),
                dma,
                dma((slices,)),
                dma((slices,)),
                dma,
                dma((4,)),
                dma((2,)),
                dma((HOME + 1, 4)),
                dma((2,)),
                pltpu.SemaphoreType.REGULAR,
            ],
            compiler_params=pltpu.CompilerParams(
                collective_id=0, has_side_effects=True, vmem_limit_bytes=56 * 2**20
            ),
            cost_estimate=pl.CostEstimate(flops=flops, bytes_accessed=2**21, transcendentals=2**18),
        )(phase, tilt, intensity, *constants)

    placed = (P("depth", "row", "col"), P(), P(None, "row", "col"))
    return jax.shard_map(
        body,
        mesh=mesh,
        in_specs=placed,
        out_specs=(P("depth", "row", "col"), P(None, "depth", None, "row", "col")),
        check_vma=False,
    )
```

```python
import functools
import math

import jax
import jax.numpy as jnp
import numpy as np
from jax import lax
from jax.experimental import pallas as pl
from jax.experimental.pallas import tpu as pltpu
from jax.sharding import PartitionSpec as P

HALO = 32
FRESNEL = 64
WIDTH = 32
OWN = 4
RUN = 4
ROWS = 256
HOME = 2
MESH = pl.DeviceIdType.MESH
F32 = jnp.float32
BF16 = jnp.bfloat16


def taps(offset):
    offset = offset.astype(np.float64)
    dist = np.maximum(np.abs(offset) - 0.5 * HALO, 0.0)
    profile = np.cos(np.pi * dist / (HALO + 2.0))
    weight = profile * profile / math.sqrt(FRESNEL)
    angle = np.pi * offset * offset / FRESNEL
    inside = np.abs(offset) <= HALO
    re = np.where(inside, np.cos(angle) * weight, 0.0).astype(np.float32)
    im = np.where(inside, np.sin(angle) * weight, 0.0).astype(np.float32)
    return re, im


def halves(matrix):
    high = matrix.astype(BF16)
    low = (matrix - high.astype(np.float32)).astype(BF16)
    return high, low


def matrices():
    i = np.arange(ROWS)
    re, im = taps(i[None, :] - i[:, None])
    row_high, row_low = halves(np.concatenate([re, im], axis=1))

    lines = []
    for o in range(2):
        out = WIDTH * o + np.arange(WIDTH)
        top, low = [], []
        for i in range(4):
            re, im = taps(out[:, None] - (WIDTH * (i - 1) + np.arange(WIDTH))[None, :])
            top += [re, -im]
            low += [im, re]
        lines += [np.concatenate(top, 1), np.concatenate(low, 1)]
    pair = np.concatenate(halves(np.concatenate(lines, 0)), 0)
    return row_high, row_low, pair


def split(value):
    high = value.astype(BF16)
    return high, (value - high.astype(F32)).astype(BF16)


def dot(a, b):
    return jnp.dot(a, b, preferred_element_type=F32)


def blocks_of(value):
    for g in range(value.shape[0] // 64):
        yield value[64 * g : 64 * g + 32], value[64 * g + 32 : 64 * g + 64]


def cmul(a, b):
    out = []
    for (ar, ai), (br, bi) in zip(blocks_of(a), blocks_of(b)):
        out += [ar * br - ai * bi, ar * bi + ai * br]
    return jnp.concatenate(out, axis=0)


def cos_sin(x):
    y = x * x
    c = F32(-1.0 / math.factorial(14))
    s = F32(-1.0 / math.factorial(15))
    for n in range(6, -1, -1):
        sign = -1.0 if n % 2 else 1.0
        c = c * y + F32(sign / math.factorial(2 * n))
        s = s * y + F32(sign / math.factorial(2 * n + 1))
    return c, s * x


def kernel(
    depth, cols, y_lo, slices,
    phase_h, tilt_h, intensity_h, row_high_h, row_low_h, pair_h,
    grad, waves,
    phase, tilt, intensity, row_high, row_low, pair,
    tiles_in, levels_in, wide_out, phase_w, screens, entering, leaving, spread, work, grads,
    wave_in, grad_in, wave_out, grad_out, grad_tiles,
    load_s, tile_s, tile_r, level_s, level_r, wide_s, wide_r, halo_s, halo_r, leave_s, leave_r, wave_r,
    grads_s, grads_r, gin_r, wout_s, wout_r, gout_s, gout_r, ready,
):
    z, row, col = lax.axis_index("depth"), lax.axis_index("row"), lax.axis_index("col")
    ring = 2 * y_lo
    half = cols // ring
    rounds = slices // RUN
    rim = RUN - 1
    own_rows = 64 * OWN
    side = 64 * RUN

    loads = [
        pltpu.make_async_copy(src, dst, load_s.at[i])
        for i, (src, dst) in enumerate(
            (
                (phase_h, phase), (intensity_h, intensity), (tilt_h, tilt),
                (row_high_h, row_high), (row_low_h, row_low), (pair_h, pair),
            )
        )
    ]
    for load in loads:
        load.start()

    x = col // y_lo
    y = (row // 2) * y_lo + col % y_lo
    b = x // half
    place_x = x % half
    strip = place_x * ring + y + (place_x % 2) * (ring - 1 - 2 * y)
    hub = row % 2 == 0
    home = min(HOME, depth - 1)
    worker = hub & (z == home)
    porter = jnp.logical_not(hub) & (z == home)
    base_row = row - row % 2
    wide = z % RUN != 0

    def hub_place(tilt_index, s):
        sx = s // ring
        turn = s % ring
        hy = turn + (sx % 2) * (ring - 1 - 2 * turn)
        return (hy // y_lo) * 2, (tilt_index * half + sx) * y_lo + hy % y_lo

    def clamp(s):
        return jnp.minimum(jnp.maximum(s, 0), cols - 1)

    left = (z,) + hub_place(b, clamp(strip - 1))
    right = (z,) + hub_place(b, clamp(strip + 1))
    has_left = worker & (strip > 0)
    has_right = worker & (strip < cols - 1)

    def same(device):
        return (device[0] == z) & (device[1] == row) & (device[2] == col)

    def remote(src, dst, send, recv, device):
        return pltpu.make_async_remote_copy(
            src_ref=src, dst_ref=dst, send_sem=send, recv_sem=recv, device_id=device, device_id_type=MESH
        )

    def push(src, dst, send, recv, device):
        me = same(device)

        @pl.when(jnp.logical_not(me))
        def _():
            remote(src, dst, send, recv, device).start()

        @pl.when(me)
        def _():
            pltpu.make_async_copy(src, dst, recv).start()

    def sent(src, dst, send, recv, device):
        @pl.when(jnp.logical_not(same(device)))
        def _():
            remote(src, dst, send, recv, device).wait_send()

    def arrived(buffer, recv):
        pltpu.make_async_copy(buffer, buffer, recv).wait()

    def tile_hubs():
        for t in range(2):
            for d in range(3):
                s = col + 1 - d
                wanted = (s >= 0) & (s < cols)
                if d != 1:
                    wanted = wanted & wide
                yield t, d, wanted, (z,) + hub_place(t, clamp(s))

    def hub_tiles():
        for d in range(3):
            c = strip + d - 1
            wanted = hub & (c >= 0) & (c < cols)
            if d != 1:
                wanted = wanted & wide
            for r in range(4):
                yield wanted, (z, jnp.int32(r), clamp(c))

    barrier = pltpu.get_barrier_semaphore()

    def greet(condition, device):
        @pl.when(condition)
        def _():
            pl.semaphore_signal(barrier, inc=1, device_id=device, device_id_type=MESH)

        return condition.astype(jnp.int32)

    expected = jnp.int32(0)
    for _, _, wanted, device in tile_hubs():
        expected += greet(wanted & jnp.logical_not(same(device)), device)
    for wanted, device in hub_tiles():
        expected += greet(wanted & jnp.logical_not(same(device)), device)
    away = hub & (z != home)
    for plane in range(depth):
        if plane != home:
            greet(worker, (jnp.int32(plane), row, col))
            for r in range(4 if plane < home else 0):
                greet(worker, (jnp.int32(plane), jnp.int32(r), strip))
            greet(porter, (jnp.int32(plane), base_row, col))
    expected += away.astype(jnp.int32)
    greet(porter, (z, base_row, col))
    early = z < home
    expected += away.astype(jnp.int32) + worker.astype(jnp.int32) + 2 * early.astype(jnp.int32)
    expected += greet(has_left, left)
    expected += greet(has_right, right)

    loads[0].wait()
    loads[1].wait()
    pl.semaphore_wait(barrier, expected)

    def ready_signal(condition, device):
        @pl.when(condition)
        def _():
            pl.semaphore_signal(ready, inc=1, device_id=device, device_id_type=MESH)


    for t, d, wanted, device in tile_hubs():
        pl.when(wanted)(
            functools.partial(push, phase.at[0], tiles_in.at[d, row], tile_s.at[t, d], tile_r.at[d], device)
        )

    ready_signal(away, (jnp.int32(home), row + 1, col))
    for t in range(2):
        ready_signal(early, (jnp.int32(home),) + hub_place(t, col))

    def level_args(t):
        return intensity.at[t], levels_in.at[row], level_s.at[t], level_r, (z,) + hub_place(t, col)

    @pl.when(z == home)
    def _():
        for t in range(2):
            push(*level_args(t))

    def turn_tiles(tiles, h):
        return jnp.concatenate([tiles[2 * h], tiles[2 * h + 1]], axis=0).T

    def wide_args():
        return wide_out, phase_w.at[z], wide_s, wide_r.at[z], (jnp.int32(home), row, col)

    def own_args():
        span = pl.ds(32 * rim, 32 * OWN)
        return wide_out.at[span], phase_w.at[z, span], wide_s, wide_r.at[z], (jnp.int32(home), row, col)

    @pl.when(hub)
    def _():
        arrived(tiles_in.at[1], tile_r.at[1])
        for h in range(2):
            wide_out[32 * rim : 32 * (rim + OWN), 128 * h : 128 * h + 128] = turn_tiles(tiles_in[1], h)

        @pl.when(wide)
        def _():
            @pl.when(strip > 0)
            def _():
                arrived(tiles_in.at[0], tile_r.at[0])
                for h in range(2):
                    turned = turn_tiles(tiles_in[0], h)
                    wide_out[: 32 * rim, 128 * h : 128 * h + 128] = turned[128 - 32 * rim :]

            @pl.when(strip == 0)
            def _():
                wide_out[: 32 * rim] = jnp.zeros((32 * rim, ROWS), F32)

            @pl.when(strip < cols - 1)
            def _():
                arrived(tiles_in.at[2], tile_r.at[2])
                for h in range(2):
                    turned = turn_tiles(tiles_in[2], h)
                    wide_out[32 * (rim + OWN) :, 128 * h : 128 * h + 128] = turned[: 32 * rim]

            @pl.when(strip == cols - 1)
            def _():
                wide_out[32 * (rim + OWN) :] = jnp.zeros((32 * rim, ROWS), F32)

            push(*wide_args())

        @pl.when(jnp.logical_not(wide))
        def _():
            push(*own_args())

    for load in loads[2:]:
        load.wait()

    def row_step(value):
        high, low = split(value)
        full = dot(high, row_high[...]) + (dot(low, row_high[...]) + dot(high, row_low[...]))
        out = []
        for a, c in blocks_of(full):
            out += [a[:, :ROWS] - c[:, ROWS:], c[:, :ROWS] + a[:, ROWS:]]
        return jnp.concatenate(out, axis=0)

    def col_step(value):
        high, low = split(value)
        out = []
        for p in range(value.shape[0] // 128 - 1):
            h, l = high[128 * p : 128 * p + 256], low[128 * p : 128 * p + 256]
            both = dot(pair[...], h)
            out.append(both[:128] + (both[128:] + dot(pair[:128], l)))
        return jnp.concatenate(out, axis=0)

    def halo_copies(k):
        part = side // 2
        far_right = side + own_rows
        spans = (
            (side, far_right, left), (own_rows + part, part, right),
            (side + part, far_right + part, left), (own_rows, 0, right),
        )
        return [
            remote(
                spread.at[k, pl.ds(src, part)], spread.at[k, pl.ds(dst, part)], halo_s.at[n, k], halo_r.at[n, k], device
            )
            for n, (src, dst, device) in enumerate(spans)
        ]

    def halo_start(k):
        for n, copy in enumerate(halo_copies(k)):
            pl.when(has_right if n % 2 else has_left)(copy.start)

    def halo_wait(k, far):
        copies = halo_copies(k)[2 * far : 2 * far + 2]
        pl.when(has_right)(copies[0].wait_recv)
        pl.when(has_left)(copies[1].wait_recv)

    def halo_sent(k):
        for n, copy in enumerate(halo_copies(k)):
            pl.when(has_right if n % 2 else has_left)(copy.wait_send)

    def make_screen(j, with_rim):
        for g in range(0 if with_rim else rim, OWN + (2 * rim if with_rim else rim)):
            c, s = cos_sin(phase_w[j, 32 * g : 32 * g + 32])
            if g < rim:
                c, s = jnp.where(strip > 0, c, 0.0), jnp.where(strip > 0, s, 0.0)
            if g >= rim + OWN:
                c, s = jnp.where(strip < cols - 1, c, 0.0), jnp.where(strip < cols - 1, s, 0.0)
            screens[j, 64 * g : 64 * g + 32] = c
            screens[j, 64 * g + 32 : 64 * g + 64] = s

    def get_screen(j, with_rim):
        if with_rim:
            arrived(phase_w.at[j], wide_r.at[j])
        else:
            span = pl.ds(32 * rim, 32 * OWN)
            arrived(phase_w.at[j, span], wide_r.at[j])
        make_screen(j, with_rim)

    def screen_on(j, out):
        return screens[j, pl.ds(64 * (rim - out), 64 * (OWN + 2 * out))]

    def leave_copy(j):
        return remote(leaving.at[j], leaving.at[j], leave_s.at[j], leave_r.at[j], (z, base_row + 1, col))

    def grads_copy(j):
        return remote(grads.at[j], grads.at[j], grads_s.at[j], grads_r.at[j], (z, base_row + 1, col))

    def leave_carry(j):
        return remote(leaving.at[j], wave_in, leave_s.at[j], wave_r, (j, base_row, col))

    def grads_carry(j):
        return remote(grads.at[j], grad_in, grads_s.at[j], gin_r, (j, base_row, col))

    def leave_start(j):
        pl.when(j != home)(leave_copy(j).start)

    def grads_start(j):
        pl.when(j > home)(grads_copy(j).start)

    def wave_turn(src):
        for c in range(2):
            value = jnp.concatenate([src[64 * g + 32 * c : 64 * g + 32 * c + 32] for g in range(OWN)], axis=0)
            for h in range(2):
                turned = value[:, 128 * h : 128 * h + 128].T
                wave_out[2 * h, c] = turned[:64]
                wave_out[2 * h + 1, c] = turned[64:]
        for r in range(4):
            push(*wave_args(r))

    def wave_args(r):
        return wave_out.at[r], waves.at[b, 0], wout_s.at[r], wout_r.at[b], (z, jnp.int32(r), strip)

    def grad_turn(src, plane, slot):
        for h in range(2):
            turned = src[:, 128 * h : 128 * h + 128].T
            grad_out[slot, 2 * h] = turned[:64]
            grad_out[slot, 2 * h + 1] = turned[64:]
        for r in range(4):
            push(*grad_args(r, plane, slot))

    def grad_args(r, plane, slot):
        device = (plane, jnp.int32(r), strip)
        return grad_out.at[slot, r], grad_tiles.at[b], gout_s.at[slot, r], gout_r.at[b], device

    def next_input(i):
        return work[pl.ds(0, 64 * (OWN + 2 * (RUN - i + 1)))]

    def first_pairs(k, j, pairs, adjoint):
        wave = jnp.concatenate([col_step(spread[k, pl.ds(128 * p, 256)]) for p in pairs], axis=0)
        screen = jnp.concatenate([screens[j if adjoint else j + 1, pl.ds(128 * p, 128)] for p in pairs], axis=0)
        after = cmul(screen, wave)
        onward = row_step(after)
        for n, p in enumerate(pairs):
            work[pl.ds(128 * p, 128)] = onward[128 * n : 128 * n + 128]
            for o in range(2):
                own = 2 * p + o - rim
                if 0 <= own < OWN:
                    at = 128 * n + 64 * o
                    if adjoint:
                        entered = entering[j, pl.ds(64 * own, 64)]
                        pr, pi = wave[at : at + 32], wave[at + 32 : at + 64]
                        grads[j, pl.ds(32 * own, 32)] = -(pr * entered[32:] + pi * entered[:32])
                    else:
                        leaving[j, pl.ds(64 * own, 64)] = wave[at : at + 64]
                        entering[j + 1, pl.ds(64 * own, 64)] = after[at : at + 64]

    def own_part(value, out):
        return value[64 * out : 64 * out + own_rows]

    def forward(k, last):
        first_slice = k * RUN
        halo_start(k)
        pl.when(k > 0)(lambda: leave_start(first_slice - 1))
        get_screen(first_slice + 1, True)
        first_pairs(k, first_slice, [2], False)
        for i in range(2, RUN):
            get_screen(first_slice + i, True)
        halo_wait(k, 0)
        first_pairs(k, first_slice, [1, 3], False)
        halo_wait(k, 1)
        first_pairs(k, first_slice, [0, 4], False)
        leave_start(first_slice)
        for i in range(2, RUN + 1):
            out = RUN - i
            j = first_slice + i - 1
            wave = col_step(next_input(i))
            leaving[j] = own_part(wave, out)
            if i < RUN:
                leave_start(j)
            elif not last:
                get_screen(j + 1, False)
            if i < RUN:
                after = cmul(screen_on(j + 1, out), wave)
                entering[j + 1] = own_part(after, out)
                work[pl.ds(0, 64 * (OWN + 2 * out))] = row_step(after)
            elif not last:
                after = cmul(screen_on(j + 1, 0), wave)
                entering[j + 1] = after
                spread[k + 1, pl.ds(side, own_rows)] = row_step(after)
            else:
                arrived(levels_in, level_r)
                level = jnp.concatenate([turn_tiles(levels_in, h) for h in range(2)], axis=1)
                seed = []
                for g, (re, im) in enumerate(blocks_of(wave)):
                    misfit = 2.0 * (re * re + im * im - level[32 * g : 32 * g + 32])
                    seed += [misfit * re, -(misfit * im)]
                spread[k + 1, pl.ds(side, own_rows)] = row_step(jnp.concatenate(seed, axis=0))

    def backward(k, last):
        first_slice = (2 * rounds - k) * RUN - 1
        first_pairs(k, first_slice, [2], True)
        halo_wait(k, 0)
        first_pairs(k, first_slice, [1, 3], True)
        halo_wait(k, 1)
        first_pairs(k, first_slice, [0, 4], True)
        grads_start(first_slice)
        for i in range(2, RUN + 1):
            out = RUN - i
            j = first_slice - (i - 1)
            pulled = col_step(next_input(i))
            if i < RUN:
                work[pl.ds(0, 64 * (OWN + 2 * out))] = row_step(cmul(screen_on(j, out), pulled))
            elif not last:
                spread[k + 1, pl.ds(side, own_rows)] = row_step(cmul(screen_on(j, 0), pulled))
                halo_start(k + 1)
            parts = []
            for (pr, pi), (er, ei) in zip(blocks_of(own_part(pulled, out)), blocks_of(entering[j])):
                parts.append(-(pr * ei + pi * er))
            grads[j] = jnp.concatenate(parts, axis=0)
            if last and RUN - i <= home:
                plane = RUN - i
                if plane == home - 1:
                    pl.semaphore_wait(ready, 4 * home)
                grad_turn(grads.at[plane], jnp.int32(plane), plane)
            else:
                grads_start(j)

    @pl.when(worker)
    def _():
        @pl.when(strip == 0)
        def _():
            @pl.loop(0, 2 * rounds)
            def _(k):
                spread[k, pl.ds(0, side)] = jnp.zeros((side, ROWS), F32)

        @pl.when(strip == cols - 1)
        def _():
            @pl.loop(0, 2 * rounds)
            def _(k):
                spread[k, pl.ds(side + own_rows, side)] = jnp.zeros((side, ROWS), F32)

        row_pos = lax.broadcasted_iota(jnp.int32, (32 * OWN, ROWS), 1).astype(F32)
        col_pos = (strip * (32 * OWN) + lax.broadcasted_iota(jnp.int32, (32 * OWN, ROWS), 0)).astype(F32)
        t0, t1 = tilt[b, 0].astype(F32), tilt[b, 1].astype(F32)
        angle = 2.0 * jnp.pi * (t0 * row_pos / float(ROWS) + t1 * col_pos / float(cols * 32 * OWN))
        cos, sin = jnp.cos(angle), jnp.sin(angle)
        incident = []
        for g in range(OWN):
            incident += [cos[32 * g : 32 * g + 32], sin[32 * g : 32 * g + 32]]
        get_screen(0, False)
        start = cmul(screen_on(0, 0), jnp.concatenate(incident, axis=0))
        entering[0] = start
        spread[0, pl.ds(side, own_rows)] = row_step(start)

        def forward_round(k, carry):
            forward(k, False)
            return carry

        def backward_round(k, carry):
            backward(k, False)
            return carry

        if rounds > 1:
            lax.fori_loop(0, rounds - 1, forward_round, 0)
        forward(jnp.int32(rounds - 1), True)
        halo_start(rounds)
        leave_start(jnp.int32(slices - 1))
        wave_turn(leaving.at[home])
        if rounds > 1:
            lax.fori_loop(rounds, 2 * rounds - 1, backward_round, 0)
        backward(jnp.int32(2 * rounds - 1), True)

    @pl.when(porter)
    def _():
        pl.semaphore_wait(ready, depth - 1)

        @pl.loop(0, slices)
        def _(j):
            @pl.when(j != home)
            def _():
                leave_copy(j).wait_recv()
                leave_carry(j).start()

        @pl.loop(0, slices)
        def _(i):
            j = slices - 1 - i

            @pl.when(j > home)
            def _():
                grads_copy(j).wait_recv()
                grads_carry(j).start()

    @pl.when(away)
    def _():
        arrived(wave_in, wave_r)
        wave_turn(wave_in)

        @pl.when(z > home)
        def _():
            arrived(grad_in, gin_r)
            grad_turn(grad_in, z, 0)

    for t in range(2):
        arrived(waves.at[t, 0], wout_r.at[t])
    for t in range(2):
        arrived(grad_tiles.at[t], gout_r.at[t])
    grad[0] = grad_tiles[0] + grad_tiles[1]

    for t, d, wanted, device in tile_hubs():
        pl.when(wanted)(
            functools.partial(sent, phase.at[0], tiles_in.at[d, row], tile_s.at[t, d], tile_r.at[d], device)
        )

    @pl.when(z == home)
    def _():
        for t in range(2):
            sent(*level_args(t))

    @pl.when(hub)
    def _():
        for r in range(4):
            sent(*wave_args(r))
            for plane in range(home + 1):
                pl.when(worker)(functools.partial(sent, *grad_args(r, jnp.int32(plane), plane)))
            pl.when(z > home)(functools.partial(sent, *grad_args(r, z, 0)))
        pl.when(wide)(lambda: sent(*wide_args()))
        pl.when(jnp.logical_not(wide))(lambda: sent(*own_args()))

    @pl.when(worker)
    def _():
        @pl.loop(0, 2 * rounds)
        def _(k):
            halo_sent(k)

    @pl.when(z == home)
    def _():
        @pl.loop(0, slices)
        def _(j):
            @pl.when(j != home)
            def _():
                leave_copy(j).wait_send()
                pl.when(j > home)(grads_copy(j).wait_send)


def solution(mesh):
    depth, cols = mesh.shape["depth"], mesh.shape["col"]
    y_lo = 4 if cols % 8 == 0 else 1
    slices = depth
    rounds = 2 * slices // RUN
    reach = OWN + 2 * (RUN - 1)
    constants = [jnp.asarray(m) for m in matrices()]

    def body(phase, tilt, intensity):
        hbm = pl.BlockSpec(memory_space=pltpu.HBM)
        vmem = pl.BlockSpec(memory_space=pltpu.VMEM)
        dma = pltpu.SemaphoreType.DMA
        strip = (64 * OWN, ROWS)
        flops = 2 * 2 * slices * 64 * 7 * ROWS * (3 * 512 + 3 * 256)
        return pl.pallas_call(
            functools.partial(kernel, depth, cols, y_lo, slices),
            out_shape=(
                jax.ShapeDtypeStruct((1, 64, 128), F32),
                jax.ShapeDtypeStruct((2, 1, 2, 64, 128), F32),
            ),
            in_specs=[hbm] * 6,
            out_specs=(vmem, vmem),
            scratch_shapes=[
                pltpu.VMEM((1, 64, 128), F32),
                pltpu.SMEM((2, 2), jnp.int32),
                pltpu.VMEM((2, 64, 128), F32),
                pltpu.VMEM((ROWS, 2 * ROWS), BF16),
                pltpu.VMEM((ROWS, 2 * ROWS), BF16),
                pltpu.VMEM((256, 256), BF16),
                pltpu.VMEM((3, 4, 64, 128), F32),
                pltpu.VMEM((4, 64, 128), F32),
                pltpu.VMEM((32 * reach, ROWS), F32),
                pltpu.VMEM((slices, 32 * reach, ROWS), F32),
                pltpu.VMEM((slices, 64 * reach, ROWS), F32),
                pltpu.VMEM((slices,) + strip, F32),
                pltpu.VMEM((slices,) + strip, F32),
                pltpu.VMEM((rounds, 64 * (OWN + 2 * RUN), ROWS), F32),
                pltpu.VMEM((64 * reach, ROWS), F32),
                pltpu.VMEM((slices, 32 * OWN, ROWS), F32),
                pltpu.VMEM(strip, F32),
                pltpu.VMEM((32 * OWN, ROWS), F32),
                pltpu.VMEM((4, 2, 64, 128), F32),
                pltpu.VMEM((HOME + 1, 4, 64, 128), F32),
                pltpu.VMEM((2, 64, 128), F32),
                dma((6,)),
                dma((2, 3)),
                dma((3,)),
                dma((2,)),
                dma,
                dma,
                dma((slices,)),
                dma((4, rounds)),
                dma((4, rounds)),
                dma((slices,)),
                dma((slices,)),
                dma,
                dma((slices,)),
                dma((slices,)),
                dma,
                dma((4,)),
                dma((2,)),
                dma((HOME + 1, 4)),
                dma((2,)),
                pltpu.SemaphoreType.REGULAR,
            ],
            compiler_params=pltpu.CompilerParams(
                collective_id=0, has_side_effects=True, vmem_limit_bytes=56 * 2**20
            ),
            cost_estimate=pl.CostEstimate(flops=flops, bytes_accessed=2**21, transcendentals=2**18),
        )(phase, tilt, intensity, *constants)

    placed = (P("depth", "row", "col"), P(), P(None, "row", "col"))
    return jax.shard_map(
        body,
        mesh=mesh,
        in_specs=placed,
        out_specs=(P("depth", "row", "col"), P(None, "depth", None, "row", "col")),
        check_vma=False,
    )
```

```python
import functools
import math

import jax
import jax.numpy as jnp
import numpy as np
from jax import lax
from jax.experimental import pallas as pl
from jax.experimental.pallas import tpu as pltpu
from jax.sharding import PartitionSpec as P

HALO = 32
FRESNEL = 64
WIDTH = 32
OWN = 4
RUN = 4
ROWS = 256
HOME = 2
MESH = pl.DeviceIdType.MESH
F32 = jnp.float32
BF16 = jnp.bfloat16


def taps(offset):
    offset = offset.astype(np.float64)
    dist = np.maximum(np.abs(offset) - 0.5 * HALO, 0.0)
    profile = np.cos(np.pi * dist / (HALO + 2.0))
    weight = profile * profile / math.sqrt(FRESNEL)
    angle = np.pi * offset * offset / FRESNEL
    inside = np.abs(offset) <= HALO
    re = np.where(inside, np.cos(angle) * weight, 0.0).astype(np.float32)
    im = np.where(inside, np.sin(angle) * weight, 0.0).astype(np.float32)
    return re, im


def halves(matrix):
    high = matrix.astype(BF16)
    low = (matrix - high.astype(np.float32)).astype(BF16)
    return high, low


def matrices():
    i = np.arange(ROWS)
    re, im = taps(i[None, :] - i[:, None])
    row_high, row_low = halves(np.concatenate([re, im], axis=1))

    lines = []
    for o in range(2):
        out = WIDTH * o + np.arange(WIDTH)
        top, low = [], []
        for i in range(4):
            re, im = taps(out[:, None] - (WIDTH * (i - 1) + np.arange(WIDTH))[None, :])
            top += [re, -im]
            low += [im, re]
        lines += [np.concatenate(top, 1), np.concatenate(low, 1)]
    pair = np.concatenate(halves(np.concatenate(lines, 0)), 0)
    return row_high, row_low, pair


def split(value):
    high = value.astype(BF16)
    return high, (value - high.astype(F32)).astype(BF16)


def dot(a, b):
    return jnp.dot(a, b, preferred_element_type=F32)


def blocks_of(value):
    for g in range(value.shape[0] // 64):
        yield value[64 * g : 64 * g + 32], value[64 * g + 32 : 64 * g + 64]


def cmul(a, b):
    out = []
    for (ar, ai), (br, bi) in zip(blocks_of(a), blocks_of(b)):
        out += [ar * br - ai * bi, ar * bi + ai * br]
    return jnp.concatenate(out, axis=0)


def cos_sin(x):
    y = x * x
    c = F32(-1.0 / math.factorial(14))
    s = F32(-1.0 / math.factorial(15))
    for n in range(6, -1, -1):
        sign = -1.0 if n % 2 else 1.0
        c = c * y + F32(sign / math.factorial(2 * n))
        s = s * y + F32(sign / math.factorial(2 * n + 1))
    return c, s * x


def kernel(
    depth, cols, y_lo, slices,
    phase_h, tilt_h, intensity_h, row_high_h, row_low_h, pair_h,
    grad, waves,
    phase, tilt, intensity, row_high, row_low, pair,
    tiles_in, levels_in, wide_out, phase_w, screens, entering, leaving, spread, work, grads,
    wave_in, grad_in, wave_out, grad_out, grad_tiles,
    load_s, tile_s, tile_r, level_s, level_r, wide_s, wide_r, halo_s, halo_r, leave_s, leave_r, wave_r,
    grads_s, grads_r, gin_r, wout_s, wout_r, gout_s, gout_r, ready,
):
    z, row, col = lax.axis_index("depth"), lax.axis_index("row"), lax.axis_index("col")
    ring = 2 * y_lo
    half = cols // ring
    rounds = slices // RUN
    rim = RUN - 1
    own_rows = 64 * OWN
    side = 64 * RUN

    loads = [
        pltpu.make_async_copy(src, dst, load_s.at[i])
        for i, (src, dst) in enumerate(
            (
                (phase_h, phase), (intensity_h, intensity), (tilt_h, tilt),
                (row_high_h, row_high), (row_low_h, row_low), (pair_h, pair),
            )
        )
    ]
    for load in loads:
        load.start()

    x = col // y_lo
    y = (row // 2) * y_lo + col % y_lo
    b = x // half
    place_x = x % half
    strip = place_x * ring + y + (place_x % 2) * (ring - 1 - 2 * y)
    hub = row % 2 == 0
    home = min(HOME, depth - 1)
    worker = hub & (z == home)
    porter = jnp.logical_not(hub) & (z == home)
    base_row = row - row % 2
    wide = z % RUN != 0

    def hub_place(tilt_index, s):
        sx = s // ring
        turn = s % ring
        hy = turn + (sx % 2) * (ring - 1 - 2 * turn)
        return (hy // y_lo) * 2, (tilt_index * half + sx) * y_lo + hy % y_lo

    def clamp(s):
        return jnp.minimum(jnp.maximum(s, 0), cols - 1)

    left = (z,) + hub_place(b, clamp(strip - 1))
    right = (z,) + hub_place(b, clamp(strip + 1))
    has_left = worker & (strip > 0)
    has_right = worker & (strip < cols - 1)

    def same(device):
        return (device[0] == z) & (device[1] == row) & (device[2] == col)

    def remote(src, dst, send, recv, device):
        return pltpu.make_async_remote_copy(
            src_ref=src, dst_ref=dst, send_sem=send, recv_sem=recv, device_id=device, device_id_type=MESH
        )

    def push(src, dst, send, recv, device):
        me = same(device)

        @pl.when(jnp.logical_not(me))
        def _():
            remote(src, dst, send, recv, device).start()

        @pl.when(me)
        def _():
            pltpu.make_async_copy(src, dst, recv).start()

    def sent(src, dst, send, recv, device):
        @pl.when(jnp.logical_not(same(device)))
        def _():
            remote(src, dst, send, recv, device).wait_send()

    def arrived(buffer, recv):
        pltpu.make_async_copy(buffer, buffer, recv).wait()

    def tile_hubs():
        for t in range(2):
            for d in range(3):
                s = col + 1 - d
                wanted = (s >= 0) & (s < cols)
                if d != 1:
                    wanted = wanted & wide
                yield t, d, wanted, (z,) + hub_place(t, clamp(s))

    def hub_tiles():
        for d in range(3):
            c = strip + d - 1
            wanted = hub & (c >= 0) & (c < cols)
            if d != 1:
                wanted = wanted & wide
            for r in range(4):
                yield wanted, (z, jnp.int32(r), clamp(c))

    barrier = pltpu.get_barrier_semaphore()

    def greet(condition, device):
        @pl.when(condition)
        def _():
            pl.semaphore_signal(barrier, inc=1, device_id=device, device_id_type=MESH)

        return condition.astype(jnp.int32)

    expected = jnp.int32(0)
    for _, _, wanted, device in tile_hubs():
        expected += greet(wanted & jnp.logical_not(same(device)), device)
    for wanted, device in hub_tiles():
        expected += greet(wanted & jnp.logical_not(same(device)), device)
    away = hub & (z != home)
    for plane in range(depth):
        if plane != home:
            greet(worker, (jnp.int32(plane), row, col))
            for r in range(4 if plane < home else 0):
                greet(worker, (jnp.int32(plane), jnp.int32(r), strip))
            greet(porter, (jnp.int32(plane), base_row, col))
    expected += away.astype(jnp.int32)
    greet(porter, (z, base_row, col))
    early = z < home
    expected += away.astype(jnp.int32) + worker.astype(jnp.int32) + 2 * early.astype(jnp.int32)
    expected += greet(has_left, left)
    expected += greet(has_right, right)

    loads[0].wait()
    loads[1].wait()
    loads[2].wait()

    @pl.when(worker)
    def _():
        @pl.when(strip == 0)
        def _():
            @pl.loop(0, 2 * rounds)
            def _(k):
                spread[k, pl.ds(0, side)] = jnp.zeros((side, ROWS), F32)

        @pl.when(strip == cols - 1)
        def _():
            @pl.loop(0, 2 * rounds)
            def _(k):
                spread[k, pl.ds(side + own_rows, side)] = jnp.zeros((side, ROWS), F32)

        row_pos = lax.broadcasted_iota(jnp.int32, (32 * OWN, ROWS), 1).astype(F32)
        col_pos = (strip * (32 * OWN) + lax.broadcasted_iota(jnp.int32, (32 * OWN, ROWS), 0)).astype(F32)
        t0, t1 = tilt[b, 0].astype(F32), tilt[b, 1].astype(F32)
        angle = 2.0 * jnp.pi * (t0 * row_pos / float(ROWS) + t1 * col_pos / float(cols * 32 * OWN))
        cos, sin = jnp.cos(angle), jnp.sin(angle)
        incident = []
        for g in range(OWN):
            incident += [cos[32 * g : 32 * g + 32], sin[32 * g : 32 * g + 32]]
        entering[0] = jnp.concatenate(incident, axis=0)

    pl.semaphore_wait(barrier, expected)

    def ready_signal(condition, device):
        @pl.when(condition)
        def _():
            pl.semaphore_signal(ready, inc=1, device_id=device, device_id_type=MESH)


    for t, d, wanted, device in tile_hubs():
        pl.when(wanted)(
            functools.partial(push, phase.at[0], tiles_in.at[d, row], tile_s.at[t, d], tile_r.at[d], device)
        )

    ready_signal(away, (jnp.int32(home), row + 1, col))
    for t in range(2):
        ready_signal(early, (jnp.int32(home),) + hub_place(t, col))

    def level_args(t):
        return intensity.at[t], levels_in.at[row], level_s.at[t], level_r, (z,) + hub_place(t, col)

    @pl.when(z == home)
    def _():
        for t in range(2):
            push(*level_args(t))

    def turn_tiles(tiles, h):
        return jnp.concatenate([tiles[2 * h], tiles[2 * h + 1]], axis=0).T

    def wide_args():
        return wide_out, phase_w.at[z], wide_s, wide_r.at[z], (jnp.int32(home), row, col)

    def own_args():
        span = pl.ds(32 * rim, 32 * OWN)
        return wide_out.at[span], phase_w.at[z, span], wide_s, wide_r.at[z], (jnp.int32(home), row, col)

    @pl.when(hub)
    def _():
        arrived(tiles_in.at[1], tile_r.at[1])
        for h in range(2):
            wide_out[32 * rim : 32 * (rim + OWN), 128 * h : 128 * h + 128] = turn_tiles(tiles_in[1], h)

        @pl.when(wide)
        def _():
            @pl.when(strip > 0)
            def _():
                arrived(tiles_in.at[0], tile_r.at[0])
                for h in range(2):
                    turned = turn_tiles(tiles_in[0], h)
                    wide_out[: 32 * rim, 128 * h : 128 * h + 128] = turned[128 - 32 * rim :]

            @pl.when(strip == 0)
            def _():
                wide_out[: 32 * rim] = jnp.zeros((32 * rim, ROWS), F32)

            @pl.when(strip < cols - 1)
            def _():
                arrived(tiles_in.at[2], tile_r.at[2])
                for h in range(2):
                    turned = turn_tiles(tiles_in[2], h)
                    wide_out[32 * (rim + OWN) :, 128 * h : 128 * h + 128] = turned[: 32 * rim]

            @pl.when(strip == cols - 1)
            def _():
                wide_out[32 * (rim + OWN) :] = jnp.zeros((32 * rim, ROWS), F32)

            push(*wide_args())

        @pl.when(jnp.logical_not(wide))
        def _():
            push(*own_args())

    for load in loads[3:]:
        load.wait()

    def row_step(value):
        if value.shape[0] > 128:
            cuts = range(0, value.shape[0], 128)
            return jnp.concatenate([row_step(value[c : c + 128]) for c in cuts], axis=0)
        high, low = split(value)
        full = dot(high, row_high[...]) + (dot(low, row_high[...]) + dot(high, row_low[...]))
        out = []
        for a, c in blocks_of(full):
            out += [a[:, :ROWS] - c[:, ROWS:], c[:, :ROWS] + a[:, ROWS:]]
        return jnp.concatenate(out, axis=0)

    def col_step(value):
        high, low = split(value)
        out = []
        for p in range(value.shape[0] // 128 - 1):
            h, l = high[128 * p : 128 * p + 256], low[128 * p : 128 * p + 256]
            both = dot(pair[...], h)
            out.append(both[:128] + (both[128:] + dot(pair[:128], l)))
        return jnp.concatenate(out, axis=0)

    def halo_copies(k):
        part = side // 2
        far_right = side + own_rows
        spans = (
            (side, far_right, left), (own_rows + part, part, right),
            (side + part, far_right + part, left), (own_rows, 0, right),
        )
        return [
            remote(
                spread.at[k, pl.ds(src, part)], spread.at[k, pl.ds(dst, part)], halo_s.at[n, k], halo_r.at[n, k], device
            )
            for n, (src, dst, device) in enumerate(spans)
        ]

    def halo_start(k):
        for n, copy in enumerate(halo_copies(k)):
            pl.when(has_right if n % 2 else has_left)(copy.start)

    def halo_wait(k, far):
        copies = halo_copies(k)[2 * far : 2 * far + 2]
        pl.when(has_right)(copies[0].wait_recv)
        pl.when(has_left)(copies[1].wait_recv)

    def halo_sent(k):
        for n, copy in enumerate(halo_copies(k)):
            pl.when(has_right if n % 2 else has_left)(copy.wait_send)

    def make_screen(j, with_rim):
        for g in range(0 if with_rim else rim, OWN + (2 * rim if with_rim else rim)):
            c, s = cos_sin(phase_w[j, 32 * g : 32 * g + 32])
            if g < rim:
                c, s = jnp.where(strip > 0, c, 0.0), jnp.where(strip > 0, s, 0.0)
            if g >= rim + OWN:
                c, s = jnp.where(strip < cols - 1, c, 0.0), jnp.where(strip < cols - 1, s, 0.0)
            screens[j, 64 * g : 64 * g + 32] = c
            screens[j, 64 * g + 32 : 64 * g + 64] = s

    def get_screen(j, with_rim):
        if with_rim:
            arrived(phase_w.at[j], wide_r.at[j])
        else:
            span = pl.ds(32 * rim, 32 * OWN)
            arrived(phase_w.at[j, span], wide_r.at[j])
        make_screen(j, with_rim)

    def screen_on(j, out):
        return screens[j, pl.ds(64 * (rim - out), 64 * (OWN + 2 * out))]

    def leave_copy(j):
        return remote(leaving.at[j], leaving.at[j], leave_s.at[j], leave_r.at[j], (z, base_row + 1, col))

    def grads_copy(j):
        return remote(grads.at[j], grads.at[j], grads_s.at[j], grads_r.at[j], (z, base_row + 1, col))

    def leave_carry(j):
        return remote(leaving.at[j], wave_in, leave_s.at[j], wave_r, (j, base_row, col))

    def grads_carry(j):
        return remote(grads.at[j], grad_in, grads_s.at[j], gin_r, (j, base_row, col))

    def leave_start(j):
        pl.when(j != home)(leave_copy(j).start)

    def grads_start(j):
        pl.when(j > home)(grads_copy(j).start)

    def wave_turn(src):
        for c in range(2):
            value = jnp.concatenate([src[64 * g + 32 * c : 64 * g + 32 * c + 32] for g in range(OWN)], axis=0)
            for h in range(2):
                turned = value[:, 128 * h : 128 * h + 128].T
                wave_out[2 * h, c] = turned[:64]
                wave_out[2 * h + 1, c] = turned[64:]
        for r in range(4):
            push(*wave_args(r))

    def wave_args(r):
        return wave_out.at[r], waves.at[b, 0], wout_s.at[r], wout_r.at[b], (z, jnp.int32(r), strip)

    def grad_turn(src, plane, slot):
        for h in range(2):
            turned = src[:, 128 * h : 128 * h + 128].T
            grad_out[slot, 2 * h] = turned[:64]
            grad_out[slot, 2 * h + 1] = turned[64:]
        for r in range(4):
            push(*grad_args(r, plane, slot))

    def grad_args(r, plane, slot):
        device = (plane, jnp.int32(r), strip)
        return grad_out.at[slot, r], grad_tiles.at[b], gout_s.at[slot, r], gout_r.at[b], device

    def next_input(i):
        return work[pl.ds(0, 64 * (OWN + 2 * (RUN - i + 1)))]

    def first_pairs(k, j, pairs, adjoint):
        wave = jnp.concatenate([col_step(spread[k, pl.ds(128 * p, 256)]) for p in pairs], axis=0)
        screen = jnp.concatenate([screens[j if adjoint else j + 1, pl.ds(128 * p, 128)] for p in pairs], axis=0)
        after = cmul(screen, wave)
        onward = row_step(after)
        for n, p in enumerate(pairs):
            work[pl.ds(128 * p, 128)] = onward[128 * n : 128 * n + 128]
            for o in range(2):
                own = 2 * p + o - rim
                if 0 <= own < OWN:
                    at = 128 * n + 64 * o
                    if adjoint:
                        entered = entering[j, pl.ds(64 * own, 64)]
                        pr, pi = wave[at : at + 32], wave[at + 32 : at + 64]
                        grads[j, pl.ds(32 * own, 32)] = -(pr * entered[32:] + pi * entered[:32])
                    else:
                        leaving[j, pl.ds(64 * own, 64)] = wave[at : at + 64]
                        entering[j + 1, pl.ds(64 * own, 64)] = after[at : at + 64]

    def own_part(value, out):
        return value[64 * out : 64 * out + own_rows]

    def forward(k, last):
        first_slice = k * RUN
        halo_start(k)
        pl.when(k > 0)(lambda: leave_start(first_slice - 1))
        get_screen(first_slice + 1, True)
        first_pairs(k, first_slice, [2], False)
        for i in range(2, RUN):
            get_screen(first_slice + i, True)
        halo_wait(k, 0)
        first_pairs(k, first_slice, [1, 3], False)
        halo_wait(k, 1)
        first_pairs(k, first_slice, [0, 4], False)
        leave_start(first_slice)
        for i in range(2, RUN + 1):
            out = RUN - i
            j = first_slice + i - 1
            if i == RUN and not last:
                get_screen(j + 1, False)
                for p in range(2):
                    span = pl.ds(128 * p, 128)
                    wave = col_step(work[pl.ds(128 * p, 256)])
                    leaving[j, span] = wave
                    after = cmul(screens[j + 1, pl.ds(64 * rim + 128 * p, 128)], wave)
                    entering[j + 1, span] = after
                    spread[k + 1, pl.ds(side + 128 * p, 128)] = row_step(after)
                continue
            wave = col_step(next_input(i))
            leaving[j] = own_part(wave, out)
            if i < RUN:
                leave_start(j)
            if i < RUN:
                after = cmul(screen_on(j + 1, out), wave)
                entering[j + 1] = own_part(after, out)
                work[pl.ds(0, 64 * (OWN + 2 * out))] = row_step(after)
            else:
                arrived(levels_in, level_r)
                level = jnp.concatenate([turn_tiles(levels_in, h) for h in range(2)], axis=1)
                seed = []
                for g, (re, im) in enumerate(blocks_of(wave)):
                    misfit = 2.0 * (re * re + im * im - level[32 * g : 32 * g + 32])
                    seed += [misfit * re, -(misfit * im)]
                spread[k + 1, pl.ds(side, own_rows)] = row_step(jnp.concatenate(seed, axis=0))

    def backward(k, last):
        first_slice = (2 * rounds - k) * RUN - 1
        first_pairs(k, first_slice, [2], True)
        halo_wait(k, 0)
        first_pairs(k, first_slice, [1, 3], True)
        halo_wait(k, 1)
        first_pairs(k, first_slice, [0, 4], True)
        grads_start(first_slice)
        for i in range(2, RUN + 1):
            out = RUN - i
            j = first_slice - (i - 1)
            if i == RUN and not last:
                for p in range(2):
                    pulled = col_step(work[pl.ds(128 * p, 256)])
                    onward = row_step(cmul(screens[j, pl.ds(64 * rim + 128 * p, 128)], pulled))
                    spread[k + 1, pl.ds(side + 128 * p, 128)] = onward
                    parts = []
                    for (pr, pi), (er, ei) in zip(blocks_of(pulled), blocks_of(entering[j, pl.ds(128 * p, 128)])):
                        parts.append(-(pr * ei + pi * er))
                    grads[j, pl.ds(64 * p, 64)] = jnp.concatenate(parts, axis=0)
                halo_start(k + 1)
                grads_start(j)
                continue
            pulled = col_step(next_input(i))
            if i < RUN:
                work[pl.ds(0, 64 * (OWN + 2 * out))] = row_step(cmul(screen_on(j, out), pulled))
            parts = []
            for (pr, pi), (er, ei) in zip(blocks_of(own_part(pulled, out)), blocks_of(entering[j])):
                parts.append(-(pr * ei + pi * er))
            grads[j] = jnp.concatenate(parts, axis=0)
            if last and RUN - i <= home:
                plane = RUN - i
                if plane == home - 1:
                    pl.semaphore_wait(ready, 4 * home)
                grad_turn(grads.at[plane], jnp.int32(plane), plane)
            else:
                grads_start(j)

    @pl.when(worker)
    def _():
        get_screen(0, False)
        start = cmul(screen_on(0, 0), entering[0])
        entering[0] = start
        spread[0, pl.ds(side, own_rows)] = row_step(start)

        def forward_round(k, carry):
            forward(k, False)
            return carry

        def backward_round(k, carry):
            backward(k, False)
            return carry

        if rounds > 1:
            lax.fori_loop(0, rounds - 1, forward_round, 0)
        forward(jnp.int32(rounds - 1), True)
        halo_start(rounds)
        leave_start(jnp.int32(slices - 1))
        wave_turn(leaving.at[home])
        if rounds > 1:
            lax.fori_loop(rounds, 2 * rounds - 1, backward_round, 0)
        backward(jnp.int32(2 * rounds - 1), True)

    @pl.when(porter)
    def _():
        pl.semaphore_wait(ready, depth - 1)

        @pl.loop(0, slices)
        def _(j):
            @pl.when(j != home)
            def _():
                leave_copy(j).wait_recv()
                leave_carry(j).start()

        @pl.loop(0, slices)
        def _(i):
            j = slices - 1 - i

            @pl.when(j > home)
            def _():
                grads_copy(j).wait_recv()
                grads_carry(j).start()

    @pl.when(away)
    def _():
        arrived(wave_in, wave_r)
        wave_turn(wave_in)

        @pl.when(z > home)
        def _():
            arrived(grad_in, gin_r)
            grad_turn(grad_in, z, 0)

    for t in range(2):
        arrived(waves.at[t, 0], wout_r.at[t])
    for t in range(2):
        arrived(grad_tiles.at[t], gout_r.at[t])
    grad[0] = grad_tiles[0] + grad_tiles[1]

    for t, d, wanted, device in tile_hubs():
        pl.when(wanted)(
            functools.partial(sent, phase.at[0], tiles_in.at[d, row], tile_s.at[t, d], tile_r.at[d], device)
        )

    @pl.when(z == home)
    def _():
        for t in range(2):
            sent(*level_args(t))

    @pl.when(hub)
    def _():
        for r in range(4):
            sent(*wave_args(r))
            for plane in range(home + 1):
                pl.when(worker)(functools.partial(sent, *grad_args(r, jnp.int32(plane), plane)))
            pl.when(z > home)(functools.partial(sent, *grad_args(r, z, 0)))
        pl.when(wide)(lambda: sent(*wide_args()))
        pl.when(jnp.logical_not(wide))(lambda: sent(*own_args()))

    @pl.when(worker)
    def _():
        @pl.loop(0, 2 * rounds)
        def _(k):
            halo_sent(k)

    @pl.when(z == home)
    def _():
        @pl.loop(0, slices)
        def _(j):
            @pl.when(j != home)
            def _():
                leave_copy(j).wait_send()
                pl.when(j > home)(grads_copy(j).wait_send)


def solution(mesh):
    depth, cols = mesh.shape["depth"], mesh.shape["col"]
    y_lo = 4 if cols % 8 == 0 else 1
    slices = depth
    rounds = 2 * slices // RUN
    reach = OWN + 2 * (RUN - 1)
    constants = [jnp.asarray(m) for m in matrices()]

    def body(phase, tilt, intensity):
        hbm = pl.BlockSpec(memory_space=pltpu.HBM)
        vmem = pl.BlockSpec(memory_space=pltpu.VMEM)
        dma = pltpu.SemaphoreType.DMA
        strip = (64 * OWN, ROWS)
        flops = 2 * 2 * slices * 64 * 7 * ROWS * (3 * 512 + 3 * 256)
        return pl.pallas_call(
            functools.partial(kernel, depth, cols, y_lo, slices),
            out_shape=(
                jax.ShapeDtypeStruct((1, 64, 128), F32),
                jax.ShapeDtypeStruct((2, 1, 2, 64, 128), F32),
            ),
            in_specs=[hbm] * 6,
            out_specs=(vmem, vmem),
            scratch_shapes=[
                pltpu.VMEM((1, 64, 128), F32),
                pltpu.SMEM((2, 2), jnp.int32),
                pltpu.VMEM((2, 64, 128), F32),
                pltpu.VMEM((ROWS, 2 * ROWS), BF16),
                pltpu.VMEM((ROWS, 2 * ROWS), BF16),
                pltpu.VMEM((256, 256), BF16),
                pltpu.VMEM((3, 4, 64, 128), F32),
                pltpu.VMEM((4, 64, 128), F32),
                pltpu.VMEM((32 * reach, ROWS), F32),
                pltpu.VMEM((slices, 32 * reach, ROWS), F32),
                pltpu.VMEM((slices, 64 * reach, ROWS), F32),
                pltpu.VMEM((slices,) + strip, F32),
                pltpu.VMEM((slices,) + strip, F32),
                pltpu.VMEM((rounds, 64 * (OWN + 2 * RUN), ROWS), F32),
                pltpu.VMEM((64 * reach, ROWS), F32),
                pltpu.VMEM((slices, 32 * OWN, ROWS), F32),
                pltpu.VMEM(strip, F32),
                pltpu.VMEM((32 * OWN, ROWS), F32),
                pltpu.VMEM((4, 2, 64, 128), F32),
                pltpu.VMEM((HOME + 1, 4, 64, 128), F32),
                pltpu.VMEM((2, 64, 128), F32),
                dma((6,)),
                dma((2, 3)),
                dma((3,)),
                dma((2,)),
                dma,
                dma,
                dma((slices,)),
                dma((4, rounds)),
                dma((4, rounds)),
                dma((slices,)),
                dma((slices,)),
                dma,
                dma((slices,)),
                dma((slices,)),
                dma,
                dma((4,)),
                dma((2,)),
                dma((HOME + 1, 4)),
                dma((2,)),
                pltpu.SemaphoreType.REGULAR,
            ],
            compiler_params=pltpu.CompilerParams(
                collective_id=0, has_side_effects=True, vmem_limit_bytes=56 * 2**20
            ),
            cost_estimate=pl.CostEstimate(flops=flops, bytes_accessed=2**21, transcendentals=2**18),
        )(phase, tilt, intensity, *constants)

    placed = (P("depth", "row", "col"), P(), P(None, "row", "col"))
    return jax.shard_map(
        body,
        mesh=mesh,
        in_specs=placed,
        out_specs=(P("depth", "row", "col"), P(None, "depth", None, "row", "col")),
        check_vma=False,
    )
```

```python
import functools
import math

import jax
import jax.numpy as jnp
import numpy as np
from jax import lax
from jax.experimental import pallas as pl
from jax.experimental.pallas import tpu as pltpu
from jax.sharding import PartitionSpec as P

HALO = 32
FRESNEL = 64
WIDTH = 32
OWN = 4
RUN = 4
ROWS = 256
HOME = 2
MESH = pl.DeviceIdType.MESH
F32 = jnp.float32
BF16 = jnp.bfloat16


def taps(offset):
    offset = offset.astype(np.float64)
    dist = np.maximum(np.abs(offset) - 0.5 * HALO, 0.0)
    profile = np.cos(np.pi * dist / (HALO + 2.0))
    weight = profile * profile / math.sqrt(FRESNEL)
    angle = np.pi * offset * offset / FRESNEL
    inside = np.abs(offset) <= HALO
    re = np.where(inside, np.cos(angle) * weight, 0.0).astype(np.float32)
    im = np.where(inside, np.sin(angle) * weight, 0.0).astype(np.float32)
    return re, im


def halves(matrix):
    high = matrix.astype(BF16)
    low = (matrix - high.astype(np.float32)).astype(BF16)
    return high, low


def matrices():
    i = np.arange(ROWS)
    re, im = taps(i[None, :] - i[:, None])
    row_high, row_low = halves(np.concatenate([re, im], axis=1))

    lines = []
    for o in range(2):
        out = WIDTH * o + np.arange(WIDTH)
        top, low = [], []
        for i in range(4):
            re, im = taps(out[:, None] - (WIDTH * (i - 1) + np.arange(WIDTH))[None, :])
            top += [re, -im]
            low += [im, re]
        lines += [np.concatenate(top, 1), np.concatenate(low, 1)]
    pair = np.concatenate(halves(np.concatenate(lines, 0)), 0)
    return row_high, row_low, pair


def split(value):
    high = value.astype(BF16)
    return high, (value - high.astype(F32)).astype(BF16)


def dot(a, b):
    return jnp.dot(a, b, preferred_element_type=F32)


def blocks_of(value):
    for g in range(value.shape[0] // 64):
        yield value[64 * g : 64 * g + 32], value[64 * g + 32 : 64 * g + 64]


def cmul(a, b):
    out = []
    for (ar, ai), (br, bi) in zip(blocks_of(a), blocks_of(b)):
        out += [ar * br - ai * bi, ar * bi + ai * br]
    return jnp.concatenate(out, axis=0)


def cos_sin(x):
    y = x * x
    c = F32(-1.0 / math.factorial(14))
    s = F32(-1.0 / math.factorial(15))
    for n in range(6, -1, -1):
        sign = -1.0 if n % 2 else 1.0
        c = c * y + F32(sign / math.factorial(2 * n))
        s = s * y + F32(sign / math.factorial(2 * n + 1))
    return c, s * x


def kernel(
    depth, cols, y_lo, slices,
    phase_h, tilt_h, intensity_h, row_high_h, row_low_h, pair_h,
    grad, waves,
    phase, tilt, intensity, row_high, row_low, pair,
    tiles_in, levels_in, wide_out, phase_w, screens, entering, leaving, spread, work, grads,
    wave_in, grad_in, wave_out, grad_out, grad_tiles,
    load_s, tile_s, tile_r, level_s, level_r, wide_s, wide_r, halo_s, halo_r, leave_s, leave_r, wave_r,
    grads_s, grads_r, gin_r, wout_s, wout_r, gout_s, gout_r, ready,
):
    z, row, col = lax.axis_index("depth"), lax.axis_index("row"), lax.axis_index("col")
    ring = 2 * y_lo
    half = cols // ring
    rounds = slices // RUN
    rim = RUN - 1
    own_rows = 64 * OWN
    side = 64 * RUN

    loads = [
        pltpu.make_async_copy(src, dst, load_s.at[i])
        for i, (src, dst) in enumerate(
            (
                (phase_h, phase), (intensity_h, intensity), (tilt_h, tilt),
                (row_high_h, row_high), (row_low_h, row_low), (pair_h, pair),
            )
        )
    ]
    for load in loads:
        load.start()

    x = col // y_lo
    y = (row // 2) * y_lo + col % y_lo
    b = x // half
    place_x = x % half
    strip = place_x * ring + y + (place_x % 2) * (ring - 1 - 2 * y)
    hub = row % 2 == 0
    home = min(HOME, depth - 1)
    worker = hub & (z == home)
    porter = jnp.logical_not(hub) & (z == home)
    base_row = row - row % 2
    wide = z % RUN != 0

    def hub_place(tilt_index, s):
        sx = s // ring
        turn = s % ring
        hy = turn + (sx % 2) * (ring - 1 - 2 * turn)
        return (hy // y_lo) * 2, (tilt_index * half + sx) * y_lo + hy % y_lo

    def clamp(s):
        return jnp.minimum(jnp.maximum(s, 0), cols - 1)

    left = (z,) + hub_place(b, clamp(strip - 1))
    right = (z,) + hub_place(b, clamp(strip + 1))
    has_left = worker & (strip > 0)
    has_right = worker & (strip < cols - 1)

    def same(device):
        return (device[0] == z) & (device[1] == row) & (device[2] == col)

    def remote(src, dst, send, recv, device):
        return pltpu.make_async_remote_copy(
            src_ref=src, dst_ref=dst, send_sem=send, recv_sem=recv, device_id=device, device_id_type=MESH
        )

    def push(src, dst, send, recv, device):
        me = same(device)

        @pl.when(jnp.logical_not(me))
        def _():
            remote(src, dst, send, recv, device).start()

        @pl.when(me)
        def _():
            pltpu.make_async_copy(src, dst, recv).start()

    def sent(src, dst, send, recv, device):
        @pl.when(jnp.logical_not(same(device)))
        def _():
            remote(src, dst, send, recv, device).wait_send()

    def arrived(buffer, recv):
        pltpu.make_async_copy(buffer, buffer, recv).wait()

    def tile_hubs():
        for t in range(2):
            for d in range(3):
                s = col + 1 - d
                wanted = (s >= 0) & (s < cols)
                if d != 1:
                    wanted = wanted & wide
                yield t, d, wanted, (z,) + hub_place(t, clamp(s))

    def hub_tiles():
        for d in range(3):
            c = strip + d - 1
            wanted = hub & (c >= 0) & (c < cols)
            if d != 1:
                wanted = wanted & wide
            for r in range(4):
                yield wanted, (z, jnp.int32(r), clamp(c))

    barrier = pltpu.get_barrier_semaphore()

    def greet(condition, device):
        @pl.when(condition)
        def _():
            pl.semaphore_signal(barrier, inc=1, device_id=device, device_id_type=MESH)

        return condition.astype(jnp.int32)

    expected = jnp.int32(0)
    for _, _, wanted, device in tile_hubs():
        expected += greet(wanted & jnp.logical_not(same(device)), device)
    for wanted, device in hub_tiles():
        expected += greet(wanted & jnp.logical_not(same(device)), device)
    away = hub & (z != home)
    for plane in range(depth):
        if plane != home:
            greet(worker, (jnp.int32(plane), row, col))
            for r in range(4 if plane < home else 0):
                greet(worker, (jnp.int32(plane), jnp.int32(r), strip))
            greet(porter, (jnp.int32(plane), base_row, col))
    expected += away.astype(jnp.int32)
    greet(porter, (z, base_row, col))
    early = z < home
    expected += away.astype(jnp.int32) + worker.astype(jnp.int32) + 2 * early.astype(jnp.int32)
    expected += greet(has_left, left)
    expected += greet(has_right, right)

    loads[0].wait()
    loads[1].wait()
    loads[2].wait()

    @pl.when(worker)
    def _():
        @pl.when(strip == 0)
        def _():
            @pl.loop(0, 2 * rounds)
            def _(k):
                spread[k, pl.ds(0, side)] = jnp.zeros((side, ROWS), F32)

        @pl.when(strip == cols - 1)
        def _():
            @pl.loop(0, 2 * rounds)
            def _(k):
                spread[k, pl.ds(side + own_rows, side)] = jnp.zeros((side, ROWS), F32)

        row_pos = lax.broadcasted_iota(jnp.int32, (32 * OWN, ROWS), 1).astype(F32)
        col_pos = (strip * (32 * OWN) + lax.broadcasted_iota(jnp.int32, (32 * OWN, ROWS), 0)).astype(F32)
        t0, t1 = tilt[b, 0].astype(F32), tilt[b, 1].astype(F32)
        angle = 2.0 * jnp.pi * (t0 * row_pos / float(ROWS) + t1 * col_pos / float(cols * 32 * OWN))
        cos, sin = jnp.cos(angle), jnp.sin(angle)
        incident = []
        for g in range(OWN):
            incident += [cos[32 * g : 32 * g + 32], sin[32 * g : 32 * g + 32]]
        entering[0] = jnp.concatenate(incident, axis=0)

    pl.semaphore_wait(barrier, expected)

    def ready_signal(condition, device):
        @pl.when(condition)
        def _():
            pl.semaphore_signal(ready, inc=1, device_id=device, device_id_type=MESH)


    for t, d, wanted, device in tile_hubs():
        pl.when(wanted)(
            functools.partial(push, phase.at[0], tiles_in.at[d, row], tile_s.at[t, d], tile_r.at[d], device)
        )

    ready_signal(away, (jnp.int32(home), row + 1, col))
    for t in range(2):
        ready_signal(early, (jnp.int32(home),) + hub_place(t, col))

    def level_args(t):
        return intensity.at[t], levels_in.at[row], level_s.at[t], level_r, (z,) + hub_place(t, col)

    @pl.when(z == home)
    def _():
        for t in range(2):
            push(*level_args(t))

    def turn_tiles(tiles, h):
        return jnp.concatenate([tiles[2 * h], tiles[2 * h + 1]], axis=0).T

    def wide_args():
        return wide_out, phase_w.at[z], wide_s, wide_r.at[z], (jnp.int32(home), row, col)

    def own_args():
        span = pl.ds(32 * rim, 32 * OWN)
        return wide_out.at[span], phase_w.at[z, span], wide_s, wide_r.at[z], (jnp.int32(home), row, col)

    @pl.when(hub)
    def _():
        arrived(tiles_in.at[1], tile_r.at[1])
        for h in range(2):
            wide_out[32 * rim : 32 * (rim + OWN), 128 * h : 128 * h + 128] = turn_tiles(tiles_in[1], h)

        @pl.when(wide)
        def _():
            @pl.when(strip > 0)
            def _():
                arrived(tiles_in.at[0], tile_r.at[0])
                for h in range(2):
                    turned = turn_tiles(tiles_in[0], h)
                    wide_out[: 32 * rim, 128 * h : 128 * h + 128] = turned[128 - 32 * rim :]

            @pl.when(strip == 0)
            def _():
                wide_out[: 32 * rim] = jnp.zeros((32 * rim, ROWS), F32)

            @pl.when(strip < cols - 1)
            def _():
                arrived(tiles_in.at[2], tile_r.at[2])
                for h in range(2):
                    turned = turn_tiles(tiles_in[2], h)
                    wide_out[32 * (rim + OWN) :, 128 * h : 128 * h + 128] = turned[: 32 * rim]

            @pl.when(strip == cols - 1)
            def _():
                wide_out[32 * (rim + OWN) :] = jnp.zeros((32 * rim, ROWS), F32)

            push(*wide_args())

        @pl.when(jnp.logical_not(wide))
        def _():
            push(*own_args())

    for load in loads[3:]:
        load.wait()

    def row_step(value):
        if value.shape[0] > 64:
            cuts = range(0, value.shape[0], 64)
            return jnp.concatenate([row_step(value[c : c + 64]) for c in cuts], axis=0)
        high, low = split(value)
        full = dot(high, row_high[...]) + (dot(low, row_high[...]) + dot(high, row_low[...]))
        out = []
        for a, c in blocks_of(full):
            out += [a[:, :ROWS] - c[:, ROWS:], c[:, :ROWS] + a[:, ROWS:]]
        return jnp.concatenate(out, axis=0)

    def col_step(value):
        high, low = split(value)
        out = []
        for p in range(value.shape[0] // 128 - 1):
            h, l = high[128 * p : 128 * p + 256], low[128 * p : 128 * p + 256]
            both = dot(pair[...], h)
            out.append(both[:128] + (both[128:] + dot(pair[:128], l)))
        return jnp.concatenate(out, axis=0)

    def halo_copies(k):
        part = side // 2
        far_right = side + own_rows
        spans = (
            (side, far_right, left), (own_rows + part, part, right),
            (side + part, far_right + part, left), (own_rows, 0, right),
        )
        return [
            remote(
                spread.at[k, pl.ds(src, part)], spread.at[k, pl.ds(dst, part)], halo_s.at[n, k], halo_r.at[n, k], device
            )
            for n, (src, dst, device) in enumerate(spans)
        ]

    def halo_start(k):
        for n, copy in enumerate(halo_copies(k)):
            pl.when(has_right if n % 2 else has_left)(copy.start)

    def halo_wait(k, far):
        copies = halo_copies(k)[2 * far : 2 * far + 2]
        pl.when(has_right)(copies[0].wait_recv)
        pl.when(has_left)(copies[1].wait_recv)

    def halo_sent(k):
        for n, copy in enumerate(halo_copies(k)):
            pl.when(has_right if n % 2 else has_left)(copy.wait_send)

    def make_screen(j, with_rim):
        for g in range(0 if with_rim else rim, OWN + (2 * rim if with_rim else rim)):
            c, s = cos_sin(phase_w[j, 32 * g : 32 * g + 32])
            if g < rim:
                c, s = jnp.where(strip > 0, c, 0.0), jnp.where(strip > 0, s, 0.0)
            if g >= rim + OWN:
                c, s = jnp.where(strip < cols - 1, c, 0.0), jnp.where(strip < cols - 1, s, 0.0)
            screens[j, 64 * g : 64 * g + 32] = c
            screens[j, 64 * g + 32 : 64 * g + 64] = s

    def get_screen(j, with_rim):
        if with_rim:
            arrived(phase_w.at[j], wide_r.at[j])
        else:
            span = pl.ds(32 * rim, 32 * OWN)
            arrived(phase_w.at[j, span], wide_r.at[j])
        make_screen(j, with_rim)

    def screen_on(j, out):
        return screens[j, pl.ds(64 * (rim - out), 64 * (OWN + 2 * out))]

    def leave_copy(j):
        return remote(leaving.at[j], leaving.at[j], leave_s.at[j], leave_r.at[j], (z, base_row + 1, col))

    def grads_copy(j):
        return remote(grads.at[j], grads.at[j], grads_s.at[j], grads_r.at[j], (z, base_row + 1, col))

    def leave_carry(j):
        return remote(leaving.at[j], wave_in, leave_s.at[j], wave_r, (j, base_row, col))

    def grads_carry(j):
        return remote(grads.at[j], grad_in, grads_s.at[j], gin_r, (j, base_row, col))

    def leave_start(j):
        pl.when(j != home)(leave_copy(j).start)

    def grads_start(j):
        pl.when(j > home)(grads_copy(j).start)

    def wave_turn(src):
        for c in range(2):
            value = jnp.concatenate([src[64 * g + 32 * c : 64 * g + 32 * c + 32] for g in range(OWN)], axis=0)
            for h in range(2):
                turned = value[:, 128 * h : 128 * h + 128].T
                wave_out[2 * h, c] = turned[:64]
                wave_out[2 * h + 1, c] = turned[64:]
        for r in range(4):
            push(*wave_args(r))

    def wave_args(r):
        return wave_out.at[r], waves.at[b, 0], wout_s.at[r], wout_r.at[b], (z, jnp.int32(r), strip)

    def grad_turn(src, plane, slot):
        for h in range(2):
            turned = src[:, 128 * h : 128 * h + 128].T
            grad_out[slot, 2 * h] = turned[:64]
            grad_out[slot, 2 * h + 1] = turned[64:]
        for r in range(4):
            push(*grad_args(r, plane, slot))

    def grad_args(r, plane, slot):
        device = (plane, jnp.int32(r), strip)
        return grad_out.at[slot, r], grad_tiles.at[b], gout_s.at[slot, r], gout_r.at[b], device

    def next_input(i):
        return work[pl.ds(0, 64 * (OWN + 2 * (RUN - i + 1)))]

    def first_pairs(k, j, pairs, adjoint):
        wave = jnp.concatenate([col_step(spread[k, pl.ds(128 * p, 256)]) for p in pairs], axis=0)
        screen = jnp.concatenate([screens[j if adjoint else j + 1, pl.ds(128 * p, 128)] for p in pairs], axis=0)
        after = cmul(screen, wave)
        onward = row_step(after)
        for n, p in enumerate(pairs):
            work[pl.ds(128 * p, 128)] = onward[128 * n : 128 * n + 128]
            for o in range(2):
                own = 2 * p + o - rim
                if 0 <= own < OWN:
                    at = 128 * n + 64 * o
                    if adjoint:
                        entered = entering[j, pl.ds(64 * own, 64)]
                        pr, pi = wave[at : at + 32], wave[at + 32 : at + 64]
                        grads[j, pl.ds(32 * own, 32)] = -(pr * entered[32:] + pi * entered[:32])
                    else:
                        leaving[j, pl.ds(64 * own, 64)] = wave[at : at + 64]
                        entering[j + 1, pl.ds(64 * own, 64)] = after[at : at + 64]

    def own_part(value, out):
        return value[64 * out : 64 * out + own_rows]

    def forward(k, last):
        first_slice = k * RUN
        halo_start(k)
        pl.when(k > 0)(lambda: leave_start(first_slice - 1))
        get_screen(first_slice + 1, True)
        first_pairs(k, first_slice, [2], False)
        for i in range(2, RUN):
            get_screen(first_slice + i, True)
        halo_wait(k, 0)
        first_pairs(k, first_slice, [1, 3], False)
        halo_wait(k, 1)
        first_pairs(k, first_slice, [0, 4], False)
        leave_start(first_slice)
        for i in range(2, RUN + 1):
            out = RUN - i
            j = first_slice + i - 1
            if i == RUN and not last:
                get_screen(j + 1, False)
                for p in range(2):
                    span = pl.ds(128 * p, 128)
                    wave = col_step(work[pl.ds(128 * p, 256)])
                    leaving[j, span] = wave
                    after = cmul(screens[j + 1, pl.ds(64 * rim + 128 * p, 128)], wave)
                    entering[j + 1, span] = after
                    spread[k + 1, pl.ds(side + 128 * p, 128)] = row_step(after)
                continue
            wave = col_step(next_input(i))
            leaving[j] = own_part(wave, out)
            if i < RUN:
                leave_start(j)
            if i < RUN:
                after = cmul(screen_on(j + 1, out), wave)
                entering[j + 1] = own_part(after, out)
                work[pl.ds(0, 64 * (OWN + 2 * out))] = row_step(after)
            else:
                arrived(levels_in, level_r)
                level = jnp.concatenate([turn_tiles(levels_in, h) for h in range(2)], axis=1)
                seed = []
                for g, (re, im) in enumerate(blocks_of(wave)):
                    misfit = 2.0 * (re * re + im * im - level[32 * g : 32 * g + 32])
                    seed += [misfit * re, -(misfit * im)]
                spread[k + 1, pl.ds(side, own_rows)] = row_step(jnp.concatenate(seed, axis=0))

    def backward(k, last):
        first_slice = (2 * rounds - k) * RUN - 1
        first_pairs(k, first_slice, [2], True)
        halo_wait(k, 0)
        first_pairs(k, first_slice, [1, 3], True)
        halo_wait(k, 1)
        first_pairs(k, first_slice, [0, 4], True)
        grads_start(first_slice)
        for i in range(2, RUN + 1):
            out = RUN - i
            j = first_slice - (i - 1)
            if i == RUN and not last:
                for p in range(2):
                    pulled = col_step(work[pl.ds(128 * p, 256)])
                    onward = row_step(cmul(screens[j, pl.ds(64 * rim + 128 * p, 128)], pulled))
                    spread[k + 1, pl.ds(side + 128 * p, 128)] = onward
                    parts = []
                    for (pr, pi), (er, ei) in zip(blocks_of(pulled), blocks_of(entering[j, pl.ds(128 * p, 128)])):
                        parts.append(-(pr * ei + pi * er))
                    grads[j, pl.ds(64 * p, 64)] = jnp.concatenate(parts, axis=0)
                halo_start(k + 1)
                grads_start(j)
                continue
            pulled = col_step(next_input(i))
            if i < RUN:
                work[pl.ds(0, 64 * (OWN + 2 * out))] = row_step(cmul(screen_on(j, out), pulled))
            parts = []
            for (pr, pi), (er, ei) in zip(blocks_of(own_part(pulled, out)), blocks_of(entering[j])):
                parts.append(-(pr * ei + pi * er))
            grads[j] = jnp.concatenate(parts, axis=0)
            if last and RUN - i <= home:
                plane = RUN - i
                if plane == home - 1:
                    pl.semaphore_wait(ready, 4 * home)
                grad_turn(grads.at[plane], jnp.int32(plane), plane)
            else:
                grads_start(j)

    @pl.when(worker)
    def _():
        get_screen(0, False)
        start = cmul(screen_on(0, 0), entering[0])
        entering[0] = start
        spread[0, pl.ds(side, own_rows)] = row_step(start)

        def forward_round(k, carry):
            forward(k, False)
            return carry

        def backward_round(k, carry):
            backward(k, False)
            return carry

        if rounds > 1:
            lax.fori_loop(0, rounds - 1, forward_round, 0)
        forward(jnp.int32(rounds - 1), True)
        halo_start(rounds)
        leave_start(jnp.int32(slices - 1))
        wave_turn(leaving.at[home])
        if rounds > 1:
            lax.fori_loop(rounds, 2 * rounds - 1, backward_round, 0)
        backward(jnp.int32(2 * rounds - 1), True)

    @pl.when(porter)
    def _():
        pl.semaphore_wait(ready, depth - 1)

        @pl.loop(0, slices)
        def _(j):
            @pl.when(j != home)
            def _():
                leave_copy(j).wait_recv()
                leave_carry(j).start()

        @pl.loop(0, slices)
        def _(i):
            j = slices - 1 - i

            @pl.when(j > home)
            def _():
                grads_copy(j).wait_recv()
                grads_carry(j).start()

    @pl.when(away)
    def _():
        arrived(wave_in, wave_r)
        wave_turn(wave_in)

        @pl.when(z > home)
        def _():
            arrived(grad_in, gin_r)
            grad_turn(grad_in, z, 0)

    for t in range(2):
        arrived(waves.at[t, 0], wout_r.at[t])
    for t in range(2):
        arrived(grad_tiles.at[t], gout_r.at[t])
    grad[0] = grad_tiles[0] + grad_tiles[1]

    for t, d, wanted, device in tile_hubs():
        pl.when(wanted)(
            functools.partial(sent, phase.at[0], tiles_in.at[d, row], tile_s.at[t, d], tile_r.at[d], device)
        )

    @pl.when(z == home)
    def _():
        for t in range(2):
            sent(*level_args(t))

    @pl.when(hub)
    def _():
        for r in range(4):
            sent(*wave_args(r))
            for plane in range(home + 1):
                pl.when(worker)(functools.partial(sent, *grad_args(r, jnp.int32(plane), plane)))
            pl.when(z > home)(functools.partial(sent, *grad_args(r, z, 0)))
        pl.when(wide)(lambda: sent(*wide_args()))
        pl.when(jnp.logical_not(wide))(lambda: sent(*own_args()))

    @pl.when(worker)
    def _():
        @pl.loop(0, 2 * rounds)
        def _(k):
            halo_sent(k)

    @pl.when(z == home)
    def _():
        @pl.loop(0, slices)
        def _(j):
            @pl.when(j != home)
            def _():
                leave_copy(j).wait_send()
                pl.when(j > home)(grads_copy(j).wait_send)


def solution(mesh):
    depth, cols = mesh.shape["depth"], mesh.shape["col"]
    y_lo = 4 if cols % 8 == 0 else 1
    slices = depth
    rounds = 2 * slices // RUN
    reach = OWN + 2 * (RUN - 1)
    constants = [jnp.asarray(m) for m in matrices()]

    def body(phase, tilt, intensity):
        hbm = pl.BlockSpec(memory_space=pltpu.HBM)
        vmem = pl.BlockSpec(memory_space=pltpu.VMEM)
        dma = pltpu.SemaphoreType.DMA
        strip = (64 * OWN, ROWS)
        flops = 2 * 2 * slices * 64 * 7 * ROWS * (3 * 512 + 3 * 256)
        return pl.pallas_call(
            functools.partial(kernel, depth, cols, y_lo, slices),
            out_shape=(
                jax.ShapeDtypeStruct((1, 64, 128), F32),
                jax.ShapeDtypeStruct((2, 1, 2, 64, 128), F32),
            ),
            in_specs=[hbm] * 6,
            out_specs=(vmem, vmem),
            scratch_shapes=[
                pltpu.VMEM((1, 64, 128), F32),
                pltpu.SMEM((2, 2), jnp.int32),
                pltpu.VMEM((2, 64, 128), F32),
                pltpu.VMEM((ROWS, 2 * ROWS), BF16),
                pltpu.VMEM((ROWS, 2 * ROWS), BF16),
                pltpu.VMEM((256, 256), BF16),
                pltpu.VMEM((3, 4, 64, 128), F32),
                pltpu.VMEM((4, 64, 128), F32),
                pltpu.VMEM((32 * reach, ROWS), F32),
                pltpu.VMEM((slices, 32 * reach, ROWS), F32),
                pltpu.VMEM((slices, 64 * reach, ROWS), F32),
                pltpu.VMEM((slices,) + strip, F32),
                pltpu.VMEM((slices,) + strip, F32),
                pltpu.VMEM((rounds, 64 * (OWN + 2 * RUN), ROWS), F32),
                pltpu.VMEM((64 * reach, ROWS), F32),
                pltpu.VMEM((slices, 32 * OWN, ROWS), F32),
                pltpu.VMEM(strip, F32),
                pltpu.VMEM((32 * OWN, ROWS), F32),
                pltpu.VMEM((4, 2, 64, 128), F32),
                pltpu.VMEM((HOME + 1, 4, 64, 128), F32),
                pltpu.VMEM((2, 64, 128), F32),
                dma((6,)),
                dma((2, 3)),
                dma((3,)),
                dma((2,)),
                dma,
                dma,
                dma((slices,)),
                dma((4, rounds)),
                dma((4, rounds)),
                dma((slices,)),
                dma((slices,)),
                dma,
                dma((slices,)),
                dma((slices,)),
                dma,
                dma((4,)),
                dma((2,)),
                dma((HOME + 1, 4)),
                dma((2,)),
                pltpu.SemaphoreType.REGULAR,
            ],
            compiler_params=pltpu.CompilerParams(
                collective_id=0, has_side_effects=True, vmem_limit_bytes=56 * 2**20
            ),
            cost_estimate=pl.CostEstimate(flops=flops, bytes_accessed=2**21, transcendentals=2**18),
        )(phase, tilt, intensity, *constants)

    placed = (P("depth", "row", "col"), P(), P(None, "row", "col"))
    return jax.shard_map(
        body,
        mesh=mesh,
        in_specs=placed,
        out_specs=(P("depth", "row", "col"), P(None, "depth", None, "row", "col")),
        check_vma=False,
    )
```
